32 devices in a mesh: groups: 1, seq: 32 (over z, y, x, core).
Axes of the slice: x: 2, y: 2, z: 4, core: 2. Of those that a mesh axis runs over, the one named last changes fastest.
Arguments:
- queries: bfloat16 [8192, 1280], P(('groups', 'seq')), may hold values from -8 to 8
- key_rows: bfloat16 [8192, 1280], P(('groups', 'seq')), may hold values from -8 to 8
- value_rows: bfloat16 [8192, 1280], P(('groups', 'seq')), may hold values from -8 to 8
- step_rates: float32 [2, 8192], P(None, ('groups', 'seq')), may hold values from 0.02 to 0.2
- fast_weights: float32 [3, 1280, 640], P(None, 'seq'), may hold values from -0.25 to 0.25
- momentum: float32 [3, 1280, 640], P('groups', 'seq'), may hold values from -0.18 to 0.18
- out_gain: float32 [1280], replicated, may hold values from 0.5 to 1.5
Outputs:
- layer_out: bfloat16 [8192, 1280], P(('groups', 'seq'))
- new_weights: float32 [3, 1280, 640], P('groups', 'seq')
- new_momentum: float32 [3, 1280, 640], P('groups', 'seq')
The draws below stay inside these ranges and needn't reach their ends.
All inputs are finite; a program needn't handle non-finite values.
Results may differ from the reference program's by a relative error of at most 0.0089.
Values may be sent and summed in bfloat16 or wider, within the bound.
A program may use at most 128 MiB of HBM per device.

```python
import math
import jax
import jax.numpy as jnp
from jax import lax

FAST_HEADS = 2
HEAD_DIM = 640
FAST_HIDDEN = 640
ATT_DIM = 128
WINDOW = 1024
WIDTH = 1280
ATT_HEADS = 10
ROWS = 1280
TOKENS = 8192


def pair_draw(key):
    seed_key = jax.random.fold_in(key, 11)
    query_key, row_key = jax.random.split(seed_key, 2)
    query_draw = jnp.clip(jax.random.normal(query_key, (TOKENS, WIDTH), jnp.float32), -8.0, 8.0)
    key_draw = jnp.clip(jax.random.normal(row_key, (TOKENS, WIDTH), jnp.float32), -8.0, 8.0)
    return (query_draw, key_draw)


def draw_queries(key, part):
    return pair_draw(key)[0].astype(jnp.bfloat16)


def draw_key_rows(key, part):
    return pair_draw(key)[1].astype(jnp.bfloat16)


def raised(values, rng, source, target, parts, factor):
    owner, partner = [(jnp.arange(values.shape[dim]) // (values.shape[dim] // parts)).reshape([-1 if axis == dim else 1 for axis in range(values.ndim)]) for dim in (source, target)]
    chosen = jax.random.permutation(rng, parts)[partner]
    strong = (owner == chosen) | (owner == (partner + parts // 2) % parts)
    return jnp.where(strong, factor * values, values)


def block_levels(key, dims, cuts, low, top_value):
    gain = 1.0
    for dim, parts in cuts:
        heights = jax.random.uniform(jax.random.fold_in(jax.random.fold_in(key, 6), dim), (parts,), jnp.float32, low / len(cuts), top_value / len(cuts))
        gain = gain * jnp.repeat(jnp.exp(heights), dims[dim] // parts).reshape((-1,) + (1,) * (len(dims) - 1 - dim))
    return gain


def gaussian(stream_key, extent, scale, most, shards=(), kind=jnp.bfloat16):
    result = jax.random.normal(stream_key, extent, jnp.float32) * scale
    if len(shards) > 0:
        result = block_levels(stream_key, extent, shards, -0.22, 0.18) * result
    return jnp.clip(result, min=-most, max=most).astype(kind)


def noise_with(own_key, shape, spread, limit, cuts, heavy, kind=jnp.bfloat16):
    entries = spread * jax.random.normal(own_key, shape, jnp.float32)
    if cuts:
        entries = entries * block_levels(own_key, shape, cuts, -0.22, 0.18)
    return jnp.clip(raised(entries, jax.random.fold_in(own_key, 3), *heavy), -limit, limit).astype(kind)


def setup_inputs(seed: int = 0, part: int = 0) -> dict:
    seeds = jax.random.split(jax.random.key(seed), 8)
    own_keys = jax.random.split(jax.random.fold_in(seeds[7], part), 8)
    queries = draw_queries(jax.random.fold_in(jax.random.fold_in(seeds[7], part), 71), part)
    key_rows = draw_key_rows(jax.random.fold_in(jax.random.fold_in(seeds[7], part), 71), part)
    value_rows = noise_with(own_keys[2], (TOKENS, WIDTH), 1.0, 8.0, ((0, 32),), (0, 1, 32, 2.75))
    step_rates = jnp.clip(jnp.exp(math.log(0.2) - 2.3025851 * jax.random.uniform(own_keys[3], (FAST_HEADS, TOKENS), jnp.float32) ** block_levels(own_keys[3], (FAST_HEADS, TOKENS), ((1, 32),), -0.2, 0.2)), 0.02, 0.2)
    fast_weights = gaussian(seeds[4], (3, ROWS, HEAD_DIM), HEAD_DIM ** -0.5, 0.25, ((1, 32),), jnp.float32)
    momentum = gaussian(own_keys[5], (3, ROWS, HEAD_DIM), 0.03, 0.18, ((1, 32),), jnp.float32)
    out_gain = jnp.clip(1.0 + 0.1 * jax.random.normal(seeds[6], (WIDTH,), jnp.float32), 0.5, 1.5)
    return dict(queries=queries, key_rows=key_rows, value_rows=value_rows, step_rates=step_rates, fast_weights=fast_weights, momentum=momentum, out_gain=out_gain)


def silu_slope(values_in):
    sigmoid_val = jax.nn.sigmoid(values_in)
    return sigmoid_val * (1.0 + values_in * (1.0 - sigmoid_val))

def row_product(left_side, right_side):
    return lax.dot_general(left_side, right_side, (((1,), (1,)), ((), ())), preferred_element_type=jnp.float32)

def token_product(left_side, right_side):
    return lax.dot_general(left_side, right_side, (((0,), (0,)), ((), ())), preferred_element_type=jnp.float32)

def reference(queries, key_rows, value_rows, step_rates, fast_weights, momentum, out_gain):
    weight_copy = fast_weights.astype(jnp.bfloat16)
    grad_scale = 1.0 / math.sqrt(TOKENS)
    gate_list, up_list, down_list = ([], [], [])
    for head_idx in range(FAST_HEADS):
        col_lo = head_idx * HEAD_DIM
        row_lo = head_idx * FAST_HIDDEN
        key_head = key_rows[:, col_lo:col_lo + HEAD_DIM]
        value_head = value_rows[:, col_lo:col_lo + HEAD_DIM]
        key_gate = row_product(key_head, weight_copy[0, row_lo:row_lo + FAST_HIDDEN])
        key_up = row_product(key_head, weight_copy[1, row_lo:row_lo + FAST_HIDDEN])
        key_hidden = (jax.nn.silu(key_gate) * key_up).astype(jnp.bfloat16)
        out_grad = (-grad_scale * step_rates[head_idx][:, None] * value_head.astype(jnp.float32)).astype(jnp.bfloat16)
        hidden_grad = row_product(out_grad, weight_copy[2, row_lo:row_lo + FAST_HIDDEN])
        gate_grad = (hidden_grad * key_up * silu_slope(key_gate)).astype(jnp.bfloat16)
        up_grad = (hidden_grad * jax.nn.silu(key_gate)).astype(jnp.bfloat16)
        gate_list.append(token_product(gate_grad, key_head))
        up_list.append(token_product(up_grad, key_head))
        down_list.append(token_product(key_hidden, out_grad))
    gradient = jnp.stack([jnp.concatenate(gate_list, 0), jnp.concatenate(up_list, 0), jnp.concatenate(down_list, 0)])
    new_momentum = 0.9 * momentum + gradient
    moved_rows = fast_weights - new_momentum
    keep_norm = jnp.sqrt(lax.optimization_barrier(jnp.mean(fast_weights * fast_weights, axis=-1, keepdims=True)))
    new_weights = moved_rows * keep_norm * lax.rsqrt(lax.optimization_barrier(jnp.mean(moved_rows * moved_rows, axis=-1, keepdims=True)) + 1e-06)
    applied = new_weights.astype(jnp.bfloat16)
    fast_list = []
    for head_idx in range(FAST_HEADS):
        col_lo = head_idx * HEAD_DIM
        row_lo = head_idx * FAST_HIDDEN
        query_head = queries[:, col_lo:col_lo + HEAD_DIM]
        query_gate = row_product(query_head, applied[0, row_lo:row_lo + FAST_HIDDEN])
        query_up = row_product(query_head, applied[1, row_lo:row_lo + FAST_HIDDEN])
        query_hidden = (jax.nn.silu(query_gate) * query_up).astype(jnp.bfloat16)
        fast_out = jnp.dot(query_hidden, applied[2, row_lo:row_lo + FAST_HIDDEN], preferred_element_type=jnp.float32)
        fast_normed = fast_out * lax.rsqrt(lax.optimization_barrier(jnp.mean(fast_out * fast_out, axis=-1, keepdims=True)) + 1e-06) * out_gain[col_lo:col_lo + HEAD_DIM]
        fast_list.append(fast_normed)
    fast_all = jnp.concatenate(fast_list, axis=1)
    block_rows = min(TOKENS, 512)
    key_padded = jnp.concatenate([jnp.zeros((WINDOW, WIDTH), jnp.bfloat16), key_rows], axis=0)
    value_padded = jnp.concatenate([jnp.zeros((WINDOW, WIDTH), jnp.bfloat16), value_rows], axis=0)

    def one_block(block_start):
        query_block = lax.dynamic_slice_in_dim(queries, block_start, block_rows, 0)
        key_block = lax.dynamic_slice_in_dim(key_padded, block_start, block_rows + WINDOW, 0)
        value_block = lax.dynamic_slice_in_dim(value_padded, block_start, block_rows + WINDOW, 0)
        query_heads = query_block.reshape(block_rows, ATT_HEADS, ATT_DIM).astype(jnp.float32)
        key_heads = key_block.reshape(block_rows + WINDOW, ATT_HEADS, ATT_DIM).astype(jnp.float32)
        value_heads = value_block.reshape(block_rows + WINDOW, ATT_HEADS, ATT_DIM).astype(jnp.float32)
        scores = jnp.einsum('qhd,khd->hqk', query_heads, key_heads) / math.sqrt(ATT_DIM)
        query_pos = block_start + jnp.arange(block_rows, dtype=jnp.int32)
        key_pos = block_start - WINDOW + jnp.arange(block_rows + WINDOW, dtype=jnp.int32)
        allowed = (key_pos[None, :] <= query_pos[:, None]) & (key_pos[None, :] > query_pos[:, None] - WINDOW) & (key_pos[None, :] >= 0)
        scores = jnp.where(allowed[None], scores, -jnp.inf)
        top_score = lax.optimization_barrier(jnp.max(scores, axis=-1, keepdims=True))
        exp_scores = jnp.exp(scores - top_score)
        att_probs = (exp_scores / lax.optimization_barrier(jnp.sum(exp_scores, axis=-1, keepdims=True))).astype(jnp.bfloat16)
        attended = jnp.einsum('hqk,khd->qhd', att_probs.astype(jnp.float32), value_heads)
        att_normed = attended * lax.rsqrt(lax.optimization_barrier(jnp.mean(attended * attended, axis=-1, keepdims=True)) + 1e-06)
        return att_normed.reshape(block_rows, WIDTH)
    block_starts = jnp.arange(TOKENS // block_rows, dtype=jnp.int32) * block_rows
    att_all = lax.map(one_block, block_starts).reshape(TOKENS, WIDTH)
    layer_out = (fast_all + att_all).astype(jnp.bfloat16)
    return (layer_out, new_weights, new_momentum)
```

```python
import functools
import math

import jax
import jax.numpy as jnp
from jax import lax
from jax.experimental import pallas as pl
from jax.experimental.pallas import tpu as pltpu
from jax.sharding import PartitionSpec as P

ATT_DIM = 128
WINDOW = 1024


def silu_slope(values_in):
    sigmoid_val = jax.nn.sigmoid(values_in)
    return sigmoid_val * (1.0 + values_in * (1.0 - sigmoid_val))


def row_product(left_side, right_side):
    return lax.dot_general(
        left_side, right_side, (((1,), (1,)), ((), ())), preferred_element_type=jnp.float32
    )


def token_product(left_side, right_side):
    return lax.dot_general(
        left_side, right_side, (((0,), (0,)), ((), ())), preferred_element_type=jnp.float32
    )


def attention_kernel(tile, base_ref, q_ref, k_ref, v_ref, o_ref):
    tokens = q_ref.shape[0]
    span = tile + WINDOW
    base = base_ref[0]
    row = lax.broadcasted_iota(jnp.int32, (tile, span), 0)
    col = lax.broadcasted_iota(jnp.int32, (tile, span), 1)
    near = (col > row) & (col <= row + WINDOW)
    for lo in range(0, tokens, tile):
        scores = row_product(q_ref[lo : lo + tile, :], k_ref[lo : lo + span, :])
        scores = scores * (1.0 / math.sqrt(ATT_DIM))
        allowed = near & (col >= WINDOW - base - lo)
        scores = jnp.where(allowed, scores, -jnp.inf)
        exp_scores = jnp.exp(scores - jnp.max(scores, axis=-1, keepdims=True))
        total = jnp.sum(exp_scores, axis=-1, keepdims=True)
        attended = jnp.dot(
            exp_scores.astype(jnp.bfloat16),
            v_ref[lo : lo + span, :],
            preferred_element_type=jnp.float32,
        ) / total
        mean = jnp.mean(attended * attended, axis=-1, keepdims=True)
        o_ref[lo : lo + tile, :] = attended * lax.rsqrt(mean + 1e-06)


def window_attention(base, q, k, v):
    tokens, width = q.shape
    keys = k.shape[0]
    tile = min(256, tokens)
    heads = width // ATT_DIM
    work = heads * tokens * (tile + WINDOW)
    return pl.pallas_call(
        functools.partial(attention_kernel, tile),
        out_shape=jax.ShapeDtypeStruct((tokens, width), jnp.float32),
        grid=(heads,),
        in_specs=[
            pl.BlockSpec(memory_space=pltpu.SMEM),
            pl.BlockSpec((tokens, ATT_DIM), lambda a: (0, a)),
            pl.BlockSpec((keys, ATT_DIM), lambda a: (0, a)),
            pl.BlockSpec((keys, ATT_DIM), lambda a: (0, a)),
        ],
        out_specs=pl.BlockSpec((tokens, ATT_DIM), lambda a: (0, a)),
        compiler_params=pltpu.CompilerParams(vmem_limit_bytes=40 * 2**20),
        cost_estimate=pl.CostEstimate(
            flops=4 * work * ATT_DIM, bytes_accessed=4 * keys * width * 2, transcendentals=work
        ),
    )(base, q, k, v)


def per_device(queries, key_rows, value_rows, step_rates, fast_weights, momentum, out_gain):
    tokens = queries.shape[0]
    head_dim = fast_weights.shape[2]
    size = lax.axis_size("seq")
    me = lax.axis_index("seq")
    first_core = me % 2 == 0
    grad_scale = 1.0 / math.sqrt(tokens * size)
    pair = [(i, i ^ 1) for i in range(size)]
    half, quarter = size // 2, size // 4
    swap = []
    for i in range(size):
        head, m, core = i // half, (i % half) // 2, i % 2
        swap.append((i, core * half + m * 2 + head))
    same_core = [[i for i in range(size) if i % 2 == c] for c in range(2)]

    held16 = lax.ppermute(fast_weights.astype(jnp.bfloat16), "seq", swap)
    start_rows = lax.all_gather(
        held16, "seq", axis=1, tiled=True, axis_index_groups=same_core
    )

    rates = jnp.repeat(step_rates.T, head_dim, axis=1)
    out_grad = (-grad_scale * rates * value_rows.astype(jnp.float32)).astype(jnp.bfloat16)
    whole = jnp.stack([key_rows, value_rows, out_grad, queries])
    low, high = whole[:, :, :head_dim], whole[:, :, head_dim:]
    kept = jnp.where(first_core, low, high)
    came = lax.ppermute(jnp.where(first_core, high, low), "seq", pair)
    mine = jnp.concatenate(
        [jnp.where(first_core, kept, came), jnp.where(first_core, came, kept)], axis=1
    )
    keys, values, outs, asks = mine[0], mine[1], mine[2], mine[3]
    held_weights = lax.ppermute(fast_weights, "seq", swap)
    held_momentum = lax.ppermute(momentum, "seq", swap)

    reach = WINDOW // (2 * tokens)
    window = [mine[:2]]
    for hop in range(1, reach + 1):
        route = [(i, i + 2 * hop) for i in range(size - 2 * hop)]
        window.insert(0, lax.ppermute(mine[:2], "seq", route))
    window = jnp.concatenate(window, axis=1)

    key_gate = row_product(keys, start_rows[0])
    key_up = row_product(keys, start_rows[1])
    hidden_grad = row_product(outs, start_rows[2])
    key_hidden = (jax.nn.silu(key_gate) * key_up).astype(jnp.bfloat16)
    gate_grad = (hidden_grad * key_up * silu_slope(key_gate)).astype(jnp.bfloat16)
    up_grad = (hidden_grad * jax.nn.silu(key_gate)).astype(jnp.bfloat16)
    total = jnp.stack(
        [
            token_product(gate_grad, keys),
            token_product(up_grad, keys),
            token_product(key_hidden, outs),
        ],
        axis=1,
    ).astype(jnp.bfloat16)
    held_sum = lax.psum_scatter(
        total, "seq", scatter_dimension=0, tiled=True, axis_index_groups=same_core
    )
    window, total = lax.optimization_barrier((window, total))
    base = jnp.reshape((me // 2) * (2 * tokens), (1,)).astype(jnp.int32)
    att_normed = window_attention(base, asks, window[0], window[1])
    held_sum, att_normed = lax.optimization_barrier((held_sum, att_normed))

    gradient = jnp.transpose(held_sum.astype(jnp.float32), (1, 0, 2))
    new_momentum = 0.9 * held_momentum + gradient
    moved = held_weights - new_momentum
    keep_norm = jnp.sqrt(jnp.mean(held_weights * held_weights, axis=-1, keepdims=True))
    new_weights = (
        moved * keep_norm * lax.rsqrt(jnp.mean(moved * moved, axis=-1, keepdims=True) + 1e-06)
    )
    applied = lax.all_gather(
        new_weights.astype(jnp.bfloat16), "seq", axis=1, tiled=True, axis_index_groups=same_core
    )
    owned_weights = lax.ppermute(new_weights, "seq", swap)
    owned_momentum = lax.ppermute(new_momentum, "seq", swap)

    query_gate = row_product(asks, applied[0])
    query_up = row_product(asks, applied[1])
    query_hidden = (jax.nn.silu(query_gate) * query_up).astype(jnp.bfloat16)
    fast_out = jnp.dot(query_hidden, applied[2], preferred_element_type=jnp.float32)
    gain = jnp.where(first_core, out_gain[:head_dim], out_gain[head_dim:])
    fast_normed = (
        fast_out
        * lax.rsqrt(jnp.mean(fast_out * fast_out, axis=-1, keepdims=True) + 1e-06)
        * gain
    )
    layer = (fast_normed + att_normed).astype(jnp.bfloat16)
    early, late = layer[:tokens], layer[tokens:]
    stay = jnp.where(first_core, early, late)
    back = lax.ppermute(jnp.where(first_core, late, early), "seq", pair)
    layer_out = jnp.concatenate(
        [jnp.where(first_core, stay, back), jnp.where(first_core, back, stay)], axis=1
    )
    return (layer_out, owned_weights, owned_momentum)


def solution(mesh):
    placed = (
        P(("groups", "seq"), None),
        P(("groups", "seq"), None),
        P(("groups", "seq"), None),
        P(None, ("groups", "seq")),
        P(None, "seq", None),
        P("groups", "seq", None),
        P(),
    )
    return jax.shard_map(
        per_device,
        mesh=mesh,
        in_specs=placed,
        out_specs=(P(("groups", "seq"), None), P("groups", "seq", None), P("groups", "seq", None)),
        check_vma=False,
    )
```

```python
import functools
import math

import jax
import jax.numpy as jnp
from jax import lax
from jax.experimental import pallas as pl
from jax.experimental.pallas import tpu as pltpu
from jax.sharding import PartitionSpec as P

ATT_DIM = 128
WINDOW = 1024


def silu_slope(values_in):
    sigmoid_val = jax.nn.sigmoid(values_in)
    return sigmoid_val * (1.0 + values_in * (1.0 - sigmoid_val))


def row_product(left_side, right_side):
    return lax.dot_general(
        left_side, right_side, (((1,), (1,)), ((), ())), preferred_element_type=jnp.float32
    )


def token_product(left_side, right_side):
    return lax.dot_general(
        left_side, right_side, (((0,), (0,)), ((), ())), preferred_element_type=jnp.float32
    )


def attention_kernel(tile, base_ref, q_ref, k_ref, v_ref, o_ref):
    tokens = q_ref.shape[0]
    span = tile + WINDOW
    base = base_ref[0]
    row = lax.broadcasted_iota(jnp.int32, (tile, span), 0)
    col = lax.broadcasted_iota(jnp.int32, (tile, span), 1)
    near = (col > row) & (col <= row + WINDOW)
    for lo in range(0, tokens, tile):
        scores = row_product(q_ref[lo : lo + tile, :], k_ref[lo : lo + span, :])
        scores = scores * (1.0 / math.sqrt(ATT_DIM))
        allowed = near & (col >= WINDOW - base - lo)
        scores = jnp.where(allowed, scores, -jnp.inf)
        exp_scores = jnp.exp(scores - jnp.max(scores, axis=-1, keepdims=True))
        total = jnp.sum(exp_scores, axis=-1, keepdims=True)
        attended = jnp.dot(
            exp_scores.astype(jnp.bfloat16),
            v_ref[lo : lo + span, :],
            preferred_element_type=jnp.float32,
        ) / total
        mean = jnp.mean(attended * attended, axis=-1, keepdims=True)
        o_ref[lo : lo + tile, :] = attended * lax.rsqrt(mean + 1e-06)


def window_attention(base, q, k, v):
    tokens, width = q.shape
    keys = k.shape[0]
    tile = min(256, tokens)
    heads = width // ATT_DIM
    work = heads * tokens * (tile + WINDOW)
    return pl.pallas_call(
        functools.partial(attention_kernel, tile),
        out_shape=jax.ShapeDtypeStruct((tokens, width), jnp.float32),
        grid=(heads,),
        in_specs=[
            pl.BlockSpec(memory_space=pltpu.SMEM),
            pl.BlockSpec((tokens, ATT_DIM), lambda a: (0, a)),
            pl.BlockSpec((keys, ATT_DIM), lambda a: (0, a)),
            pl.BlockSpec((keys, ATT_DIM), lambda a: (0, a)),
        ],
        out_specs=pl.BlockSpec((tokens, ATT_DIM), lambda a: (0, a)),
        compiler_params=pltpu.CompilerParams(vmem_limit_bytes=40 * 2**20),
        cost_estimate=pl.CostEstimate(
            flops=4 * work * ATT_DIM, bytes_accessed=4 * keys * width * 2, transcendentals=work
        ),
    )(base, q, k, v)


MESH = pl.DeviceIdType.MESH


def group_shape(size):
    chips = size // 2
    inner = 1
    while inner * inner * 4 <= chips:
        inner *= 2
    return chips // inner, inner


def place(outer, inner):
    me = lax.axis_index("seq")
    core = lax.rem(me, 2)
    chip = lax.div(me, 2)
    return lax.div(chip, inner), lax.rem(chip, inner), lambda i, j: {"seq": (i * inner + j) * 2 + core}


def greet(outer, inner, a, b, device):
    barrier = pltpu.get_barrier_semaphore()
    for k in range(1, outer):
        peer = device(lax.rem(a + k, outer), b)
        pl.semaphore_signal(barrier, inc=1, device_id=peer, device_id_type=MESH)
    for k in range(1, inner):
        peer = device(a, lax.rem(b + k, inner))
        pl.semaphore_signal(barrier, inc=1, device_id=peer, device_id_type=MESH)
    pl.semaphore_wait(barrier, outer + inner - 2)


def gather(outer, inner, a, b, device, shard, out, local_sem, send_sem, recv_sem):
    def copy(src, slot, send, i, j):
        return pltpu.make_async_remote_copy(
            src_ref=src,
            dst_ref=out.at[:, slot],
            send_sem=send_sem.at[send],
            recv_sem=recv_sem.at[slot],
            device_id=device(i, j),
            device_id_type=MESH,
        )

    own = a * inner + b
    started = []

    def start(src, slot, i, j):
        one = copy(src, slot, len(started), i, j)
        one.start()
        started.append(one)

    for k in range(1, outer):
        start(shard, own, lax.rem(a + k, outer), b)
    for k in range(1, inner):
        start(shard, own, a, lax.rem(b + k, inner))
    mine = pltpu.make_async_copy(shard, out.at[:, own], local_sem)
    mine.start()
    for k in range(1, outer):
        slot = lax.rem(a + k, outer) * inner + b
        copy(shard, slot, 0, lax.rem(a + 1, outer), b).wait_recv()
        for n in range(1, inner):
            start(out.at[:, slot], slot, a, lax.rem(b + n, inner))
    for k in range(outer):
        for n in range(1, inner):
            slot = lax.rem(a + k, outer) * inner + lax.rem(b + n, inner)
            copy(shard, slot, 0, lax.rem(a + 1, outer), b).wait_recv()
    mine.wait()
    for one in started:
        one.wait_send()


def gather_kernel(outer, inner, shard, out, local_sem, send_sem, recv_sem):
    a, b, device = place(outer, inner)
    greet(outer, inner, a, b, device)
    gather(outer, inner, a, b, device, shard, out, local_sem, send_sem, recv_sem)


def update_kernel(
    outer, inner, part, weights, momentum, new_weights, new_momentum, out,
    near, sums, far, own16, near_send, near_recv, far_send, far_recv,
    local_sem, send_sem, recv_sem,
):
    a, b, device = place(outer, inner)
    greet(outer, inner, a, b, device)
    steps = list(range(1, outer)) + [0]
    near_copies = {}
    for j in steps:
        for k in range(1, inner):
            peer = lax.rem(b + k, inner)
            one = pltpu.make_async_remote_copy(
                src_ref=part.at[:, lax.rem(a + j, outer) * inner + peer],
                dst_ref=near.at[k - 1, j],
                send_sem=near_send.at[k - 1, j],
                recv_sem=near_recv.at[k - 1, j],
                device_id=device(a, peer),
                device_id_type=MESH,
            )
            one.start()
            near_copies[k, j] = one
    far_copies = []
    total = None
    for j in steps:
        target = lax.rem(a + j, outer)
        total = part[:, target * inner + b].astype(jnp.float32)
        for k in range(1, inner):
            near_copies[k, j].wait_recv()
            total = total + near[k - 1, j].astype(jnp.float32)
        if j:
            sums[j - 1] = total.astype(jnp.bfloat16)
            one = pltpu.make_async_remote_copy(
                src_ref=sums.at[j - 1],
                dst_ref=far.at[j - 1],
                send_sem=far_send.at[j - 1],
                recv_sem=far_recv.at[j - 1],
                device_id=device(target, b),
                device_id_type=MESH,
            )
            one.start()
            far_copies.append(one)
    for j, one in enumerate(far_copies):
        one.wait_recv()
        total = total + far[j].astype(jnp.float32)
    fast = weights[...]
    moment = 0.9 * momentum[...] + total
    new_momentum[...] = moment
    moved = fast - moment
    keep_norm = jnp.sqrt(jnp.mean(fast * fast, axis=-1, keepdims=True))
    fresh = moved * keep_norm * lax.rsqrt(jnp.mean(moved * moved, axis=-1, keepdims=True) + 1e-06)
    new_weights[...] = fresh
    own16[...] = fresh.astype(jnp.bfloat16)
    gather(outer, inner, a, b, device, own16, out, local_sem, send_sem, recv_sem)
    for one in far_copies:
        one.wait_send()
    for one in near_copies.values():
        one.wait_send()


def gather_sems(outer, inner):
    return [
        pltpu.SemaphoreType.DMA,
        pltpu.SemaphoreType.DMA((outer * inner - 1 + outer - 1 + inner,)),
        pltpu.SemaphoreType.DMA((outer * inner,)),
    ]


def gathered(shard):
    outer, inner = group_shape(lax.axis_size("seq"))
    m, rows, width = shard.shape
    vmem = pl.BlockSpec(memory_space=pltpu.VMEM)
    out = pl.pallas_call(
        functools.partial(gather_kernel, outer, inner),
        out_shape=jax.ShapeDtypeStruct((m, outer * inner, rows, width), shard.dtype),
        in_specs=[vmem],
        out_specs=vmem,
        scratch_shapes=gather_sems(outer, inner),
        compiler_params=pltpu.CompilerParams(
            collective_id=0, has_side_effects=True, vmem_limit_bytes=32 * 2**20
        ),
        cost_estimate=pl.CostEstimate(flops=0, bytes_accessed=10**8, transcendentals=0),
    )(shard)
    return out.reshape(m, outer * inner * rows, width)


def updated(part, weights, momentum):
    outer, inner = group_shape(lax.axis_size("seq"))
    m, rows, width = weights.shape
    vmem = pl.BlockSpec(memory_space=pltpu.VMEM)
    block = (m, rows, width)
    dma = pltpu.SemaphoreType.DMA
    fresh, moment, out = pl.pallas_call(
        functools.partial(update_kernel, outer, inner),
        out_shape=(
            jax.ShapeDtypeStruct(block, jnp.float32),
            jax.ShapeDtypeStruct(block, jnp.float32),
            jax.ShapeDtypeStruct((m, outer * inner, rows, width), jnp.bfloat16),
        ),
        in_specs=[vmem] * 3,
        out_specs=(vmem,) * 3,
        scratch_shapes=[
            pltpu.VMEM((inner - 1, outer) + block, jnp.bfloat16),
            pltpu.VMEM((outer - 1,) + block, jnp.bfloat16),
            pltpu.VMEM((outer - 1,) + block, jnp.bfloat16),
            pltpu.VMEM(block, jnp.bfloat16),
            dma((inner - 1, outer)),
            dma((inner - 1, outer)),
            dma((outer - 1,)),
            dma((outer - 1,)),
        ]
        + gather_sems(outer, inner),
        compiler_params=pltpu.CompilerParams(
            collective_id=1, has_side_effects=True, vmem_limit_bytes=40 * 2**20
        ),
        cost_estimate=pl.CostEstimate(flops=0, bytes_accessed=2 * 10**8, transcendentals=0),
    )(part, weights, momentum)
    return fresh, moment, out.reshape(m, outer * inner * rows, width)


def per_device(queries, key_rows, value_rows, step_rates, fast_weights, momentum, out_gain):
    tokens = queries.shape[0]
    head_dim = fast_weights.shape[2]
    size = lax.axis_size("seq")
    me = lax.axis_index("seq")
    first_core = me % 2 == 0
    grad_scale = 1.0 / math.sqrt(tokens * size)
    pair = [(i, i ^ 1) for i in range(size)]
    half, quarter = size // 2, size // 4
    swap = []
    for i in range(size):
        head, m, core = i // half, (i % half) // 2, i % 2
        swap.append((i, core * half + m * 2 + head))

    held16 = lax.ppermute(fast_weights.astype(jnp.bfloat16), "seq", swap)
    start_rows = gathered(held16)

    rates = jnp.repeat(step_rates.T, head_dim, axis=1)
    out_grad = (-grad_scale * rates * value_rows.astype(jnp.float32)).astype(jnp.bfloat16)
    whole = jnp.stack([key_rows, value_rows, out_grad, queries])
    low, high = whole[:, :, :head_dim], whole[:, :, head_dim:]
    kept = jnp.where(first_core, low, high)
    came = lax.ppermute(jnp.where(first_core, high, low), "seq", pair)
    mine = jnp.concatenate(
        [jnp.where(first_core, kept, came), jnp.where(first_core, came, kept)], axis=1
    )
    keys, values, outs, asks = mine[0], mine[1], mine[2], mine[3]
    held_weights = lax.ppermute(fast_weights, "seq", swap)
    held_momentum = lax.ppermute(momentum, "seq", swap)

    reach = WINDOW // (2 * tokens)
    window = [mine[:2]]
    for hop in range(1, reach + 1):
        route = [(i, i + 2 * hop) for i in range(size - 2 * hop)]
        window.insert(0, lax.ppermute(mine[:2], "seq", route))
    window = jnp.concatenate(window, axis=1)

    key_gate = row_product(keys, start_rows[0])
    key_up = row_product(keys, start_rows[1])
    hidden_grad = row_product(outs, start_rows[2])
    key_hidden = (jax.nn.silu(key_gate) * key_up).astype(jnp.bfloat16)
    gate_grad = (hidden_grad * key_up * silu_slope(key_gate)).astype(jnp.bfloat16)
    up_grad = (hidden_grad * jax.nn.silu(key_gate)).astype(jnp.bfloat16)
    rows = fast_weights.shape[1]
    total = jnp.stack(
        [
            token_product(gate_grad, keys),
            token_product(up_grad, keys),
            token_product(key_hidden, outs),
        ]
    ).astype(jnp.bfloat16).reshape(3, half, rows, head_dim)
    new_weights, new_momentum, applied = updated(total, held_weights, held_momentum)
    window, applied = lax.optimization_barrier((window, applied))
    base = jnp.reshape((me // 2) * (2 * tokens), (1,)).astype(jnp.int32)
    att_normed = window_attention(base, asks, window[0], window[1])
    owned_weights = lax.ppermute(new_weights, "seq", swap)
    owned_momentum = lax.ppermute(new_momentum, "seq", swap)

    query_gate = row_product(asks, applied[0])
    query_up = row_product(asks, applied[1])
    query_hidden = (jax.nn.silu(query_gate) * query_up).astype(jnp.bfloat16)
    fast_out = jnp.dot(query_hidden, applied[2], preferred_element_type=jnp.float32)
    gain = jnp.where(first_core, out_gain[:head_dim], out_gain[head_dim:])
    fast_normed = (
        fast_out
        * lax.rsqrt(jnp.mean(fast_out * fast_out, axis=-1, keepdims=True) + 1e-06)
        * gain
    )
    layer = (fast_normed + att_normed).astype(jnp.bfloat16)
    early, late = layer[:tokens], layer[tokens:]
    stay = jnp.where(first_core, early, late)
    back = lax.ppermute(jnp.where(first_core, late, early), "seq", pair)
    layer_out = jnp.concatenate(
        [jnp.where(first_core, stay, back), jnp.where(first_core, back, stay)], axis=1
    )
    return (layer_out, owned_weights, owned_momentum)


def solution(mesh):
    placed = (
        P(("groups", "seq"), None),
        P(("groups", "seq"), None),
        P(("groups", "seq"), None),
        P(None, ("groups", "seq")),
        P(None, "seq", None),
        P("groups", "seq", None),
        P(),
    )
    return jax.shard_map(
        per_device,
        mesh=mesh,
        in_specs=placed,
        out_specs=(P(("groups", "seq"), None), P("groups", "seq", None), P("groups", "seq", None)),
        check_vma=False,
    )
```

```python
import functools
import math

import jax
import jax.numpy as jnp
from jax import lax
from jax.experimental import pallas as pl
from jax.experimental.pallas import tpu as pltpu
from jax.sharding import PartitionSpec as P

ATT_DIM = 128
WINDOW = 1024


def silu_slope(values_in):
    sigmoid_val = jax.nn.sigmoid(values_in)
    return sigmoid_val * (1.0 + values_in * (1.0 - sigmoid_val))


def row_product(left_side, right_side):
    return lax.dot_general(
        left_side, right_side, (((1,), (1,)), ((), ())), preferred_element_type=jnp.float32
    )


def token_product(left_side, right_side):
    return lax.dot_general(
        left_side, right_side, (((0,), (0,)), ((), ())), preferred_element_type=jnp.float32
    )


def attention_kernel(tile, pieces, base_ref, q_ref, *refs):
    o_ref = refs[pieces]
    keys = jnp.concatenate([ref[0] for ref in refs[:pieces]], axis=0)
    values = jnp.concatenate([ref[1] for ref in refs[:pieces]], axis=0)
    tokens = q_ref.shape[0]
    span = tile + WINDOW
    base = base_ref[0]
    row = lax.broadcasted_iota(jnp.int32, (tile, span), 0)
    col = lax.broadcasted_iota(jnp.int32, (tile, span), 1)
    near = (col > row) & (col <= row + WINDOW)
    for lo in range(0, tokens, tile):
        scores = row_product(q_ref[lo : lo + tile, :], keys[lo : lo + span])
        scores = scores * (1.0 / math.sqrt(ATT_DIM))
        allowed = near & (col >= WINDOW - base - lo)
        scores = jnp.where(allowed, scores, -jnp.inf)
        exp_scores = jnp.exp(scores - jnp.max(scores, axis=-1, keepdims=True))
        total = jnp.sum(exp_scores, axis=-1, keepdims=True)
        attended = jnp.dot(
            exp_scores.astype(jnp.bfloat16),
            values[lo : lo + span],
            preferred_element_type=jnp.float32,
        ) / total
        mean = jnp.mean(attended * attended, axis=-1, keepdims=True)
        o_ref[lo : lo + tile, :] = attended * lax.rsqrt(mean + 1e-06)


def window_attention(base, q, window):
    tokens, width = q.shape
    tile = min(256, tokens)
    heads = width // ATT_DIM
    work = heads * tokens * (tile + WINDOW)
    pair = pl.BlockSpec((2, tokens, ATT_DIM), lambda a: (0, 0, a))
    return pl.pallas_call(
        functools.partial(attention_kernel, tile, len(window)),
        out_shape=jax.ShapeDtypeStruct((tokens, width), jnp.float32),
        grid=(heads,),
        in_specs=[
            pl.BlockSpec(memory_space=pltpu.SMEM),
            pl.BlockSpec((tokens, ATT_DIM), lambda a: (0, a)),
        ]
        + [pair] * len(window),
        out_specs=pl.BlockSpec((tokens, ATT_DIM), lambda a: (0, a)),
        compiler_params=pltpu.CompilerParams(vmem_limit_bytes=40 * 2**20),
        cost_estimate=pl.CostEstimate(
            flops=4 * work * ATT_DIM,
            bytes_accessed=4 * len(window) * tokens * width,
            transcendentals=work,
        ),
    )(base, q, *window)


MESH = pl.DeviceIdType.MESH


INNER = 4


def group_shape(size):
    return size // 2 // INNER, INNER


def sides(b):
    x = b + 1 - 2 * lax.rem(b, 2)
    return x, lax.rem(b + 2, INNER), lax.rem(x + 2, INNER)


def place(outer, inner):
    me = lax.axis_index("seq")
    core = lax.rem(me, 2)
    chip = lax.div(me, 2)
    return lax.div(chip, inner), lax.rem(chip, inner), lambda i, j: {"seq": (i * inner + j) * 2 + core}


def greet(outer, inner, a, b, device):
    barrier = pltpu.get_barrier_semaphore()
    for k in range(1, outer):
        peer = device(lax.rem(a + k, outer), b)
        pl.semaphore_signal(barrier, inc=1, device_id=peer, device_id_type=MESH)
    for peer in sides(b)[:2]:
        pl.semaphore_signal(barrier, inc=1, device_id=device(a, peer), device_id_type=MESH)
    pl.semaphore_wait(barrier, outer + 1)


def gather(outer, inner, a, b, device, shard, out, local_sem, send_sem, recv_sem):
    def copy(src, slot, send, i, j):
        return pltpu.make_async_remote_copy(
            src_ref=src,
            dst_ref=out.at[:, slot],
            send_sem=send_sem.at[send],
            recv_sem=recv_sem.at[slot],
            device_id=device(i, j),
            device_id_type=MESH,
        )

    own = a * inner + b
    started = []

    def start(src, slot, i, j):
        one = copy(src, slot, len(started), i, j)
        one.start()
        started.append(one)

    x, y, across = sides(b)

    def slot_of(k, i):
        return lax.rem(a + k, outer) * inner + i

    def arrived(slot):
        copy(shard, slot, 0, a, x).wait_recv()

    def relay(k):
        source, target = ((x, y), (y, x))[k % 2]
        slot = slot_of(k, source)
        arrived(slot)
        start(out.at[:, slot], slot, a, target)

    for k in range(1, outer):
        start(shard, own, lax.rem(a + k, outer), b)
    mine = pltpu.make_async_copy(shard, out.at[:, own], local_sem)
    mine.start()
    for k in range(outer):
        slot = slot_of(k, b)
        source = shard
        if k:
            arrived(slot)
            source = out.at[:, slot]
        start(source, slot, a, x)
        start(source, slot, a, y)
        if k:
            relay(k - 1)
    relay(outer - 1)
    for k in range(outer):
        arrived(slot_of(k, (y, x)[k % 2]))
        arrived(slot_of(k, across))
    mine.wait()
    for one in started:
        one.wait_send()


def gather_kernel(outer, inner, shard, out, local_sem, send_sem, recv_sem):
    a, b, device = place(outer, inner)
    greet(outer, inner, a, b, device)
    gather(outer, inner, a, b, device, shard, out, local_sem, send_sem, recv_sem)


def update_kernel(
    outer, inner, part, weights, momentum, new_weights, new_momentum, out,
    near, mixed, sums, far, own16, near_send, near_recv, far_send, far_recv,
    local_sem, send_sem, recv_sem,
):
    a, b, device = place(outer, inner)
    greet(outer, inner, a, b, device)
    steps = list(range(1, outer)) + [0]
    x, y, across = sides(b)
    near_copies = {}

    def send_near(kind, j, src, peer):
        one = pltpu.make_async_remote_copy(
            src_ref=src,
            dst_ref=near.at[kind, j],
            send_sem=near_send.at[kind, j],
            recv_sem=near_recv.at[kind, j],
            device_id=device(a, peer),
            device_id_type=MESH,
        )
        one.start()
        near_copies[kind, j] = one

    def block(j, i):
        return lax.rem(a + j, outer) * inner + i

    for j in steps:
        first = (x, y)[j % 2]
        send_near(0, j, part.at[:, block(j, across)], first)
        send_near(1, j, part.at[:, block(j, first)], first)
    for j in steps:
        second = (y, x)[j % 2]
        near_copies[0, j].wait_recv()
        both = part[:, block(j, second)].astype(jnp.float32) + near[0, j].astype(jnp.float32)
        mixed[j] = both.astype(jnp.bfloat16)
        send_near(2, j, mixed.at[j], second)
    far_copies = []
    total = None
    for j in steps:
        target = lax.rem(a + j, outer)
        total = part[:, block(j, b)].astype(jnp.float32)
        for kind in (1, 2):
            near_copies[kind, j].wait_recv()
            total = total + near[kind, j].astype(jnp.float32)
        if j:
            sums[j - 1] = total.astype(jnp.bfloat16)
            one = pltpu.make_async_remote_copy(
                src_ref=sums.at[j - 1],
                dst_ref=far.at[j - 1],
                send_sem=far_send.at[j - 1],
                recv_sem=far_recv.at[j - 1],
                device_id=device(target, b),
                device_id_type=MESH,
            )
            one.start()
            far_copies.append(one)
    for j, one in enumerate(far_copies):
        one.wait_recv()
        total = total + far[j].astype(jnp.float32)
    fast = weights[...]
    moment = 0.9 * momentum[...] + total
    new_momentum[...] = moment
    moved = fast - moment
    keep_norm = jnp.sqrt(jnp.mean(fast * fast, axis=-1, keepdims=True))
    fresh = moved * keep_norm * lax.rsqrt(jnp.mean(moved * moved, axis=-1, keepdims=True) + 1e-06)
    new_weights[...] = fresh
    own16[...] = fresh.astype(jnp.bfloat16)
    gather(outer, inner, a, b, device, own16, out, local_sem, send_sem, recv_sem)
    for one in far_copies:
        one.wait_send()
    for one in near_copies.values():
        one.wait_send()


def gather_sems(outer, inner):
    return [
        pltpu.SemaphoreType.DMA,
        pltpu.SemaphoreType.DMA((outer - 1 + 3 * outer,)),
        pltpu.SemaphoreType.DMA((outer * inner,)),
    ]


def gathered(shard):
    outer, inner = group_shape(lax.axis_size("seq"))
    m, rows, width = shard.shape
    vmem = pl.BlockSpec(memory_space=pltpu.VMEM)
    out = pl.pallas_call(
        functools.partial(gather_kernel, outer, inner),
        out_shape=jax.ShapeDtypeStruct((m, outer * inner, rows, width), shard.dtype),
        in_specs=[vmem],
        out_specs=vmem,
        scratch_shapes=gather_sems(outer, inner),
        compiler_params=pltpu.CompilerParams(
            collective_id=0, has_side_effects=True, vmem_limit_bytes=32 * 2**20
        ),
        cost_estimate=pl.CostEstimate(flops=0, bytes_accessed=10**8, transcendentals=0),
    )(shard)
    return out.reshape(m, outer * inner * rows, width)


def updated(part, weights, momentum):
    outer, inner = group_shape(lax.axis_size("seq"))
    m, rows, width = weights.shape
    vmem = pl.BlockSpec(memory_space=pltpu.VMEM)
    block = (m, rows, width)
    dma = pltpu.SemaphoreType.DMA
    fresh, moment, out = pl.pallas_call(
        functools.partial(update_kernel, outer, inner),
        out_shape=(
            jax.ShapeDtypeStruct(block, jnp.float32),
            jax.ShapeDtypeStruct(block, jnp.float32),
            jax.ShapeDtypeStruct((m, outer * inner, rows, width), jnp.bfloat16),
        ),
        in_specs=[vmem] * 3,
        out_specs=(vmem,) * 3,
        scratch_shapes=[
            pltpu.VMEM((3, outer) + block, jnp.bfloat16),
            pltpu.VMEM((outer,) + block, jnp.bfloat16),
            pltpu.VMEM((outer - 1,) + block, jnp.bfloat16),
            pltpu.VMEM((outer - 1,) + block, jnp.bfloat16),
            pltpu.VMEM(block, jnp.bfloat16),
            dma((3, outer)),
            dma((3, outer)),
            dma((outer - 1,)),
            dma((outer - 1,)),
        ]
        + gather_sems(outer, inner),
        compiler_params=pltpu.CompilerParams(
            collective_id=1, has_side_effects=True, vmem_limit_bytes=40 * 2**20
        ),
        cost_estimate=pl.CostEstimate(flops=0, bytes_accessed=2 * 10**8, transcendentals=0),
    )(part, weights, momentum)
    return fresh, moment, out.reshape(m, outer * inner * rows, width)


def per_device(queries, key_rows, value_rows, step_rates, fast_weights, momentum, out_gain):
    tokens = queries.shape[0]
    head_dim = fast_weights.shape[2]
    size = lax.axis_size("seq")
    me = lax.axis_index("seq")
    first_core = me % 2 == 0
    grad_scale = 1.0 / math.sqrt(tokens * size)
    pair = [(i, i ^ 1) for i in range(size)]
    half, quarter = size // 2, size // 4
    swap = []
    for i in range(size):
        head, m, core = i // half, (i % half) // 2, i % 2
        swap.append((i, core * half + m * 2 + head))

    held16 = lax.ppermute(fast_weights.astype(jnp.bfloat16), "seq", swap)
    start_rows = gathered(held16)

    rates = jnp.repeat(step_rates.T, head_dim, axis=1)
    out_grad = (-grad_scale * rates * value_rows.astype(jnp.float32)).astype(jnp.bfloat16)
    whole = jnp.stack([key_rows, value_rows, out_grad, queries])
    low, high = whole[:, :, :head_dim], whole[:, :, head_dim:]
    kept = jnp.where(first_core, low, high)
    came = lax.ppermute(jnp.where(first_core, high, low), "seq", pair)
    mine = jnp.concatenate(
        [jnp.where(first_core, kept, came), jnp.where(first_core, came, kept)], axis=1
    )
    keys, values, outs, asks = mine[0], mine[1], mine[2], mine[3]
    held = lax.ppermute(jnp.stack([fast_weights, momentum]), "seq", swap)

    reach = WINDOW // (2 * tokens)
    own_pair = mine[:2]
    window = [own_pair]
    if reach == 2:
        ahead = [(i, i + 4) for i in range(size - 4)]
        beside = [(i, i ^ 2) for i in range(size)]
        distant = lax.ppermute(own_pair, "seq", ahead)
        even_chip = (me // 2) % 2 == 0
        close = lax.ppermute(jnp.where(even_chip, own_pair, distant), "seq", beside)
        window = [distant, close, own_pair]
    else:
        for hop in range(1, reach + 1):
            route = [(i, i + 2 * hop) for i in range(size - 2 * hop)]
            window.insert(0, lax.ppermute(own_pair, "seq", route))

    key_gate = row_product(keys, start_rows[0])
    key_up = row_product(keys, start_rows[1])
    hidden_grad = row_product(outs, start_rows[2])
    key_hidden = (jax.nn.silu(key_gate) * key_up).astype(jnp.bfloat16)
    gate_grad = (hidden_grad * key_up * silu_slope(key_gate)).astype(jnp.bfloat16)
    up_grad = (hidden_grad * jax.nn.silu(key_gate)).astype(jnp.bfloat16)
    rows = fast_weights.shape[1]
    total = jnp.stack(
        [
            token_product(gate_grad, keys),
            token_product(up_grad, keys),
            token_product(key_hidden, outs),
        ]
    ).astype(jnp.bfloat16).reshape(3, half, rows, head_dim)
    new_weights, new_momentum, applied = updated(total, held[0], held[1])
    asks, applied = lax.optimization_barrier((asks, applied))
    base = jnp.reshape((me // 2) * (2 * tokens), (1,)).astype(jnp.int32)
    att_normed = window_attention(base, asks, window)
    owned = lax.ppermute(jnp.stack([new_weights, new_momentum]), "seq", swap)

    query_gate = row_product(asks, applied[0])
    query_up = row_product(asks, applied[1])
    query_hidden = (jax.nn.silu(query_gate) * query_up).astype(jnp.bfloat16)
    fast_out = jnp.dot(query_hidden, applied[2], preferred_element_type=jnp.float32)
    gain = jnp.where(first_core, out_gain[:head_dim], out_gain[head_dim:])
    fast_normed = (
        fast_out
        * lax.rsqrt(jnp.mean(fast_out * fast_out, axis=-1, keepdims=True) + 1e-06)
        * gain
    )
    layer = (fast_normed + att_normed).astype(jnp.bfloat16)
    early, late = layer[:tokens], layer[tokens:]
    stay = jnp.where(first_core, early, late)
    back = lax.ppermute(jnp.where(first_core, late, early), "seq", pair)
    layer_out = jnp.concatenate(
        [jnp.where(first_core, stay, back), jnp.where(first_core, back, stay)], axis=1
    )
    return (layer_out, owned[0], owned[1])


def solution(mesh):
    placed = (
        P(("groups", "seq"), None),
        P(("groups", "seq"), None),
        P(("groups", "seq"), None),
        P(None, ("groups", "seq")),
        P(None, "seq", None),
        P("groups", "seq", None),
        P(),
    )
    return jax.shard_map(
        per_device,
        mesh=mesh,
        in_specs=placed,
        out_specs=(P(("groups", "seq"), None), P("groups", "seq", None), P("groups", "seq", None)),
        check_vma=False,
    )
```

```python
import functools
import math

import jax
import jax.numpy as jnp
from jax import lax
from jax.experimental import pallas as pl
from jax.experimental.pallas import tpu as pltpu
from jax.sharding import PartitionSpec as P

ATT_DIM = 128
WINDOW = 1024


def silu_slope(values_in):
    sigmoid_val = jax.nn.sigmoid(values_in)
    return sigmoid_val * (1.0 + values_in * (1.0 - sigmoid_val))


def row_product(left_side, right_side):
    return lax.dot_general(
        left_side, right_side, (((1,), (1,)), ((), ())), preferred_element_type=jnp.float32
    )


def token_product(left_side, right_side):
    return lax.dot_general(
        left_side, right_side, (((0,), (0,)), ((), ())), preferred_element_type=jnp.float32
    )


def attention_kernel(tile, pieces, base_ref, q_ref, *refs):
    o_ref = refs[pieces]
    keys = jnp.concatenate([ref[0] for ref in refs[:pieces]], axis=0)
    values = jnp.concatenate([ref[1] for ref in refs[:pieces]], axis=0)
    tokens = q_ref.shape[0]
    span = tile + WINDOW
    base = base_ref[0]
    row = lax.broadcasted_iota(jnp.int32, (tile, span), 0)
    col = lax.broadcasted_iota(jnp.int32, (tile, span), 1)
    near = (col > row) & (col <= row + WINDOW)
    for lo in range(0, tokens, tile):
        scores = row_product(q_ref[lo : lo + tile, :], keys[lo : lo + span])
        scores = scores * (1.0 / math.sqrt(ATT_DIM))
        allowed = near & (col >= WINDOW - base - lo)
        scores = jnp.where(allowed, scores, -jnp.inf)
        exp_scores = jnp.exp(scores - jnp.max(scores, axis=-1, keepdims=True))
        total = jnp.sum(exp_scores, axis=-1, keepdims=True)
        attended = jnp.dot(
            exp_scores.astype(jnp.bfloat16),
            values[lo : lo + span],
            preferred_element_type=jnp.float32,
        ) / total
        mean = jnp.mean(attended * attended, axis=-1, keepdims=True)
        o_ref[lo : lo + tile, :] = attended * lax.rsqrt(mean + 1e-06)


def window_attention(base, q, window):
    tokens, width = q.shape
    tile = min(256, tokens)
    heads = width // ATT_DIM
    work = heads * tokens * (tile + WINDOW)
    pair = pl.BlockSpec((2, tokens, ATT_DIM), lambda a: (0, 0, a))
    return pl.pallas_call(
        functools.partial(attention_kernel, tile, len(window)),
        out_shape=jax.ShapeDtypeStruct((tokens, width), jnp.float32),
        grid=(heads,),
        in_specs=[
            pl.BlockSpec(memory_space=pltpu.SMEM),
            pl.BlockSpec((tokens, ATT_DIM), lambda a: (0, a)),
        ]
        + [pair] * len(window),
        out_specs=pl.BlockSpec((tokens, ATT_DIM), lambda a: (0, a)),
        compiler_params=pltpu.CompilerParams(vmem_limit_bytes=40 * 2**20),
        cost_estimate=pl.CostEstimate(
            flops=4 * work * ATT_DIM,
            bytes_accessed=4 * len(window) * tokens * width,
            transcendentals=work,
        ),
    )(base, q, *window)


MESH = pl.DeviceIdType.MESH


INNER = 4


def group_shape(size):
    return size // 2 // INNER, INNER


def sides(b):
    x = b + 1 - 2 * lax.rem(b, 2)
    return x, lax.rem(b + 2, INNER), lax.rem(x + 2, INNER)


def place(outer, inner):
    me = lax.axis_index("seq")
    core = lax.rem(me, 2)
    chip = lax.div(me, 2)
    return lax.div(chip, inner), lax.rem(chip, inner), lambda i, j: {"seq": (i * inner + j) * 2 + core}


def swap_partner(outer, inner):
    me = lax.axis_index("seq")
    half = outer * inner
    head, core = lax.div(me, half), lax.rem(me, 2)
    m = lax.div(lax.rem(me, half), 2)
    return head != core, head == core, {"seq": core * half + m * 2 + head}


def trade(outer, inner, moves):
    goes, stays, partner = swap_partner(outer, inner)

    def each(do_remote, do_local):
        @pl.when(goes)
        def _():
            for src, dst, send, recv in moves:
                do_remote(
                    pltpu.make_async_remote_copy(
                        src_ref=src,
                        dst_ref=dst,
                        send_sem=send,
                        recv_sem=recv,
                        device_id=partner,
                        device_id_type=MESH,
                    )
                )

        @pl.when(stays)
        def _():
            for src, dst, send, recv in moves:
                do_local(pltpu.make_async_copy(src, dst, recv))

    each(lambda one: one.start(), lambda one: one.start())
    return lambda: each(lambda one: one.wait(), lambda one: one.wait())


def greet(outer, inner, a, b, device):
    barrier = pltpu.get_barrier_semaphore()
    goes, stays, partner = swap_partner(outer, inner)

    @pl.when(goes)
    def _():
        pl.semaphore_signal(barrier, inc=1, device_id=partner, device_id_type=MESH)

    for k in range(1, outer):
        peer = device(lax.rem(a + k, outer), b)
        pl.semaphore_signal(barrier, inc=1, device_id=peer, device_id_type=MESH)
    for peer in sides(b)[:2]:
        pl.semaphore_signal(barrier, inc=1, device_id=device(a, peer), device_id_type=MESH)

    @pl.when(goes)
    def _():
        pl.semaphore_wait(barrier, outer + 2)

    @pl.when(stays)
    def _():
        pl.semaphore_wait(barrier, outer + 1)


def gather(outer, inner, a, b, device, shard, out, local_sem, send_sem, recv_sem):
    def copy(src, slot, send, i, j):
        return pltpu.make_async_remote_copy(
            src_ref=src,
            dst_ref=out.at[:, slot],
            send_sem=send_sem.at[send],
            recv_sem=recv_sem.at[slot],
            device_id=device(i, j),
            device_id_type=MESH,
        )

    own = a * inner + b
    started = []

    def start(src, slot, i, j):
        one = copy(src, slot, len(started), i, j)
        one.start()
        started.append(one)

    x, y, across = sides(b)

    def slot_of(k, i):
        return lax.rem(a + k, outer) * inner + i

    def arrived(slot):
        copy(shard, slot, 0, a, x).wait_recv()

    def relay(k):
        source, target = ((x, y), (y, x))[k % 2]
        slot = slot_of(k, source)
        arrived(slot)
        start(out.at[:, slot], slot, a, target)

    for k in range(1, outer):
        start(shard, own, lax.rem(a + k, outer), b)
    mine = pltpu.make_async_copy(shard, out.at[:, own], local_sem)
    mine.start()
    for k in range(outer):
        slot = slot_of(k, b)
        source = shard
        if k:
            arrived(slot)
            source = out.at[:, slot]
        start(source, slot, a, x)
        start(source, slot, a, y)
        if k:
            relay(k - 1)
    relay(outer - 1)
    for k in range(outer):
        arrived(slot_of(k, (y, x)[k % 2]))
        arrived(slot_of(k, across))
    mine.wait()
    for one in started:
        one.wait_send()


def gather_kernel(outer, inner, own, out, shard, trade_sem, local_sem, send_sem, recv_sem):
    a, b, device = place(outer, inner)
    greet(outer, inner, a, b, device)
    trade(outer, inner, [(own, shard, trade_sem.at[0], trade_sem.at[1])])()
    gather(outer, inner, a, b, device, shard, out, local_sem, send_sem, recv_sem)


def update_kernel(
    outer, inner, part, own_weights, own_momentum, new_weights, new_momentum, out,
    weights, momentum, fresh_weights, fresh_momentum, trade_sem,
    near, mixed, sums, far, own16, near_send, near_recv, far_send, far_recv,
    local_sem, send_sem, recv_sem,
):
    a, b, device = place(outer, inner)
    greet(outer, inner, a, b, device)
    take = trade(
        outer,
        inner,
        [
            (own_weights, weights, trade_sem.at[0], trade_sem.at[1]),
            (own_momentum, momentum, trade_sem.at[2], trade_sem.at[3]),
        ],
    )
    steps = list(range(1, outer)) + [0]
    x, y, across = sides(b)
    near_copies = {}

    def send_near(kind, j, src, peer):
        one = pltpu.make_async_remote_copy(
            src_ref=src,
            dst_ref=near.at[kind, j],
            send_sem=near_send.at[kind, j],
            recv_sem=near_recv.at[kind, j],
            device_id=device(a, peer),
            device_id_type=MESH,
        )
        one.start()
        near_copies[kind, j] = one

    def block(j, i):
        return lax.rem(a + j, outer) * inner + i

    for j in steps:
        first = (x, y)[j % 2]
        send_near(0, j, part.at[:, block(j, across)], first)
        send_near(1, j, part.at[:, block(j, first)], first)
    for j in steps:
        second = (y, x)[j % 2]
        near_copies[0, j].wait_recv()
        both = part[:, block(j, second)].astype(jnp.float32) + near[0, j].astype(jnp.float32)
        mixed[j] = both.astype(jnp.bfloat16)
        send_near(2, j, mixed.at[j], second)
    far_copies = []
    total = None
    for j in steps:
        target = lax.rem(a + j, outer)
        total = part[:, block(j, b)].astype(jnp.float32)
        for kind in (1, 2):
            near_copies[kind, j].wait_recv()
            total = total + near[kind, j].astype(jnp.float32)
        if j:
            sums[j - 1] = total.astype(jnp.bfloat16)
            one = pltpu.make_async_remote_copy(
                src_ref=sums.at[j - 1],
                dst_ref=far.at[j - 1],
                send_sem=far_send.at[j - 1],
                recv_sem=far_recv.at[j - 1],
                device_id=device(target, b),
                device_id_type=MESH,
            )
            one.start()
            far_copies.append(one)
    for j, one in enumerate(far_copies):
        one.wait_recv()
        total = total + far[j].astype(jnp.float32)
    take()
    fast = weights[...]
    moment = 0.9 * momentum[...] + total
    fresh_momentum[...] = moment
    moved = fast - moment
    keep_norm = jnp.sqrt(jnp.mean(fast * fast, axis=-1, keepdims=True))
    fresh = moved * keep_norm * lax.rsqrt(jnp.mean(moved * moved, axis=-1, keepdims=True) + 1e-06)
    fresh_weights[...] = fresh
    own16[...] = fresh.astype(jnp.bfloat16)
    give = trade(
        outer,
        inner,
        [
            (fresh_weights, new_weights, trade_sem.at[4], trade_sem.at[5]),
            (fresh_momentum, new_momentum, trade_sem.at[6], trade_sem.at[7]),
        ],
    )
    gather(outer, inner, a, b, device, own16, out, local_sem, send_sem, recv_sem)
    give()
    for one in far_copies:
        one.wait_send()
    for one in near_copies.values():
        one.wait_send()


def gather_sems(outer, inner):
    return [
        pltpu.SemaphoreType.DMA,
        pltpu.SemaphoreType.DMA((outer - 1 + 3 * outer,)),
        pltpu.SemaphoreType.DMA((outer * inner,)),
    ]


def gathered(shard):
    outer, inner = group_shape(lax.axis_size("seq"))
    m, rows, width = shard.shape
    vmem = pl.BlockSpec(memory_space=pltpu.VMEM)
    out = pl.pallas_call(
        functools.partial(gather_kernel, outer, inner),
        out_shape=jax.ShapeDtypeStruct((m, outer * inner, rows, width), shard.dtype),
        in_specs=[vmem],
        out_specs=vmem,
        scratch_shapes=[pltpu.VMEM(shard.shape, shard.dtype), pltpu.SemaphoreType.DMA((2,))]
        + gather_sems(outer, inner),
        compiler_params=pltpu.CompilerParams(
            collective_id=0, has_side_effects=True, vmem_limit_bytes=32 * 2**20
        ),
        cost_estimate=pl.CostEstimate(flops=0, bytes_accessed=10**8, transcendentals=0),
    )(shard)
    return out.reshape(m, outer * inner * rows, width)


def updated(part, weights, momentum):
    outer, inner = group_shape(lax.axis_size("seq"))
    m, rows, width = weights.shape
    vmem = pl.BlockSpec(memory_space=pltpu.VMEM)
    block = (m, rows, width)
    dma = pltpu.SemaphoreType.DMA
    fresh, moment, out = pl.pallas_call(
        functools.partial(update_kernel, outer, inner),
        out_shape=(
            jax.ShapeDtypeStruct(block, jnp.float32),
            jax.ShapeDtypeStruct(block, jnp.float32),
            jax.ShapeDtypeStruct((m, outer * inner, rows, width), jnp.bfloat16),
        ),
        in_specs=[vmem] * 3,
        out_specs=(vmem,) * 3,
        scratch_shapes=[
            pltpu.VMEM(block, jnp.float32),
            pltpu.VMEM(block, jnp.float32),
            pltpu.VMEM(block, jnp.float32),
            pltpu.VMEM(block, jnp.float32),
            dma((8,)),
            pltpu.VMEM((3, outer) + block, jnp.bfloat16),
            pltpu.VMEM((outer,) + block, jnp.bfloat16),
            pltpu.VMEM((outer - 1,) + block, jnp.bfloat16),
            pltpu.VMEM((outer - 1,) + block, jnp.bfloat16),
            pltpu.VMEM(block, jnp.bfloat16),
            dma((3, outer)),
            dma((3, outer)),
            dma((outer - 1,)),
            dma((outer - 1,)),
        ]
        + gather_sems(outer, inner),
        compiler_params=pltpu.CompilerParams(
            collective_id=1, has_side_effects=True, vmem_limit_bytes=40 * 2**20
        ),
        cost_estimate=pl.CostEstimate(flops=0, bytes_accessed=2 * 10**8, transcendentals=0),
    )(part, weights, momentum)
    return fresh, moment, out.reshape(m, outer * inner * rows, width)


def per_device(queries, key_rows, value_rows, step_rates, fast_weights, momentum, out_gain):
    tokens = queries.shape[0]
    head_dim = fast_weights.shape[2]
    size = lax.axis_size("seq")
    me = lax.axis_index("seq")
    first_core = me % 2 == 0
    grad_scale = 1.0 / math.sqrt(tokens * size)
    pair = [(i, i ^ 1) for i in range(size)]
    half = size // 2
    start_rows = gathered(fast_weights.astype(jnp.bfloat16))

    rates = jnp.repeat(step_rates.T, head_dim, axis=1)
    out_grad = (-grad_scale * rates * value_rows.astype(jnp.float32)).astype(jnp.bfloat16)
    whole = jnp.stack([key_rows, value_rows, out_grad, queries])
    low, high = whole[:, :, :head_dim], whole[:, :, head_dim:]
    kept = jnp.where(first_core, low, high)
    came = lax.ppermute(jnp.where(first_core, high, low), "seq", pair)
    mine = jnp.concatenate(
        [jnp.where(first_core, kept, came), jnp.where(first_core, came, kept)], axis=1
    )
    keys, values, outs, asks = mine[0], mine[1], mine[2], mine[3]

    reach = WINDOW // (2 * tokens)
    own_pair = mine[:2]
    window = [own_pair]
    if reach == 2:
        ahead = [(i, i + 4) for i in range(size - 4)]
        beside = [(i, i ^ 2) for i in range(size)]
        distant = lax.ppermute(own_pair, "seq", ahead)
        even_chip = (me // 2) % 2 == 0
        close = lax.ppermute(jnp.where(even_chip, own_pair, distant), "seq", beside)
        window = [distant, close, own_pair]
    else:
        for hop in range(1, reach + 1):
            route = [(i, i + 2 * hop) for i in range(size - 2 * hop)]
            window.insert(0, lax.ppermute(own_pair, "seq", route))

    key_gate = row_product(keys, start_rows[0])
    key_up = row_product(keys, start_rows[1])
    hidden_grad = row_product(outs, start_rows[2])
    key_hidden = (jax.nn.silu(key_gate) * key_up).astype(jnp.bfloat16)
    gate_grad = (hidden_grad * key_up * silu_slope(key_gate)).astype(jnp.bfloat16)
    up_grad = (hidden_grad * jax.nn.silu(key_gate)).astype(jnp.bfloat16)
    rows = fast_weights.shape[1]
    total = jnp.stack(
        [
            token_product(gate_grad, keys),
            token_product(up_grad, keys),
            token_product(key_hidden, outs),
        ]
    ).astype(jnp.bfloat16).reshape(3, half, rows, head_dim)
    new_weights, new_momentum, applied = updated(total, fast_weights, momentum)
    asks, applied = lax.optimization_barrier((asks, applied))
    base = jnp.reshape((me // 2) * (2 * tokens), (1,)).astype(jnp.int32)
    att_normed = window_attention(base, asks, window)
    query_gate = row_product(asks, applied[0])
    query_up = row_product(asks, applied[1])
    query_hidden = (jax.nn.silu(query_gate) * query_up).astype(jnp.bfloat16)
    fast_out = jnp.dot(query_hidden, applied[2], preferred_element_type=jnp.float32)
    gain = jnp.where(first_core, out_gain[:head_dim], out_gain[head_dim:])
    fast_normed = (
        fast_out
        * lax.rsqrt(jnp.mean(fast_out * fast_out, axis=-1, keepdims=True) + 1e-06)
        * gain
    )
    layer = (fast_normed + att_normed).astype(jnp.bfloat16)
    early, late = layer[:tokens], layer[tokens:]
    stay = jnp.where(first_core, early, late)
    back = lax.ppermute(jnp.where(first_core, late, early), "seq", pair)
    layer_out = jnp.concatenate(
        [jnp.where(first_core, stay, back), jnp.where(first_core, back, stay)], axis=1
    )
    return (layer_out, new_weights, new_momentum)


def solution(mesh):
    placed = (
        P(("groups", "seq"), None),
        P(("groups", "seq"), None),
        P(("groups", "seq"), None),
        P(None, ("groups", "seq")),
        P(None, "seq", None),
        P("groups", "seq", None),
        P(),
    )
    return jax.shard_map(
        per_device,
        mesh=mesh,
        in_specs=placed,
        out_specs=(P(("groups", "seq"), None), P("groups", "seq", None), P("groups", "seq", None)),
        check_vma=False,
    )
```

```python
import functools
import math

import jax
import jax.numpy as jnp
from jax import lax
from jax.experimental import pallas as pl
from jax.experimental.pallas import tpu as pltpu
from jax.sharding import PartitionSpec as P

ATT_DIM = 128
WINDOW = 1024


def silu_slope(values_in):
    sigmoid_val = jax.nn.sigmoid(values_in)
    return sigmoid_val * (1.0 + values_in * (1.0 - sigmoid_val))


def row_product(left_side, right_side):
    return lax.dot_general(
        left_side, right_side, (((1,), (1,)), ((), ())), preferred_element_type=jnp.float32
    )


def token_product(left_side, right_side):
    return lax.dot_general(
        left_side, right_side, (((0,), (0,)), ((), ())), preferred_element_type=jnp.float32
    )


def attention_kernel(tile, pieces, base_ref, q_ref, *refs):
    o_ref = refs[pieces]
    keys = jnp.concatenate([ref[0] for ref in refs[:pieces]], axis=0)
    values = jnp.concatenate([ref[1] for ref in refs[:pieces]], axis=0)
    tokens = q_ref.shape[0]
    span = tile + WINDOW
    base = base_ref[0]
    row = lax.broadcasted_iota(jnp.int32, (tile, span), 0)
    col = lax.broadcasted_iota(jnp.int32, (tile, span), 1)
    near = (col > row) & (col <= row + WINDOW)
    for lo in range(0, tokens, tile):
        scores = row_product(q_ref[lo : lo + tile, :], keys[lo : lo + span])
        scores = scores * (1.0 / math.sqrt(ATT_DIM))
        allowed = near & (col >= WINDOW - base - lo)
        scores = jnp.where(allowed, scores, -jnp.inf)
        exp_scores = jnp.exp(scores - jnp.max(scores, axis=-1, keepdims=True))
        total = jnp.sum(exp_scores, axis=-1, keepdims=True)
        attended = jnp.dot(
            exp_scores.astype(jnp.bfloat16),
            values[lo : lo + span],
            preferred_element_type=jnp.float32,
        ) / total
        mean = jnp.mean(attended * attended, axis=-1, keepdims=True)
        o_ref[lo : lo + tile, :] = attended * lax.rsqrt(mean + 1e-06)


def window_attention(base, q, window):
    tokens, width = q.shape
    tile = min(256, tokens)
    heads = width // ATT_DIM
    work = heads * tokens * (tile + WINDOW)
    pair = pl.BlockSpec((2, tokens, ATT_DIM), lambda a: (0, 0, a))
    return pl.pallas_call(
        functools.partial(attention_kernel, tile, len(window)),
        out_shape=jax.ShapeDtypeStruct((tokens, width), jnp.float32),
        grid=(heads,),
        in_specs=[
            pl.BlockSpec(memory_space=pltpu.SMEM),
            pl.BlockSpec((tokens, ATT_DIM), lambda a: (0, a)),
        ]
        + [pair] * len(window),
        out_specs=pl.BlockSpec((tokens, ATT_DIM), lambda a: (0, a)),
        compiler_params=pltpu.CompilerParams(vmem_limit_bytes=40 * 2**20),
        cost_estimate=pl.CostEstimate(
            flops=4 * work * ATT_DIM,
            bytes_accessed=4 * len(window) * tokens * width,
            transcendentals=work,
        ),
    )(base, q, *window)


MESH = pl.DeviceIdType.MESH


INNER = 4


def group_shape(size):
    return size // 2 // INNER, INNER


def sides(b):
    x = b + 1 - 2 * lax.rem(b, 2)
    return x, lax.rem(b + 2, INNER), lax.rem(x + 2, INNER)


def place(outer, inner):
    me = lax.axis_index("seq")
    core = lax.rem(me, 2)
    chip = lax.div(me, 2)
    return lax.div(chip, inner), lax.rem(chip, inner), lambda i, j: {"seq": (i * inner + j) * 2 + core}


def swap_partner(outer, inner):
    me = lax.axis_index("seq")
    half = outer * inner
    head, core = lax.div(me, half), lax.rem(me, 2)
    m = lax.div(lax.rem(me, half), 2)
    return head != core, head == core, {"seq": core * half + m * 2 + head}


def trade(outer, inner, moves):
    goes, stays, partner = swap_partner(outer, inner)

    def each(do_remote, do_local):
        @pl.when(goes)
        def _():
            for src, dst, send, recv in moves:
                do_remote(
                    pltpu.make_async_remote_copy(
                        src_ref=src,
                        dst_ref=dst,
                        send_sem=send,
                        recv_sem=recv,
                        device_id=partner,
                        device_id_type=MESH,
                    )
                )

        @pl.when(stays)
        def _():
            for src, dst, send, recv in moves:
                do_local(pltpu.make_async_copy(src, dst, recv))

    each(lambda one: one.start(), lambda one: one.start())
    return lambda: each(lambda one: one.wait(), lambda one: one.wait())


def greet(outer, inner, a, b, device):
    barrier = pltpu.get_barrier_semaphore()
    goes, stays, partner = swap_partner(outer, inner)

    @pl.when(goes)
    def _():
        pl.semaphore_signal(barrier, inc=1, device_id=partner, device_id_type=MESH)

    for k in range(1, outer):
        peer = device(lax.rem(a + k, outer), b)
        pl.semaphore_signal(barrier, inc=1, device_id=peer, device_id_type=MESH)
    for peer in sides(b)[:2]:
        pl.semaphore_signal(barrier, inc=1, device_id=device(a, peer), device_id_type=MESH)

    @pl.when(goes)
    def _():
        pl.semaphore_wait(barrier, outer + 2)

    @pl.when(stays)
    def _():
        pl.semaphore_wait(barrier, outer + 1)


def gather(outer, inner, a, b, device, shard, out, local_sem, send_sem, recv_sem):
    def copy(src, slot, send, i, j):
        return pltpu.make_async_remote_copy(
            src_ref=src,
            dst_ref=out.at[:, slot],
            send_sem=send_sem.at[send],
            recv_sem=recv_sem.at[slot],
            device_id=device(i, j),
            device_id_type=MESH,
        )

    own = a * inner + b
    started = []

    def start(src, slot, i, j):
        one = copy(src, slot, len(started), i, j)
        one.start()
        started.append(one)

    x, y, across = sides(b)

    def slot_of(k, i):
        return lax.rem(a + k, outer) * inner + i

    def arrived(slot):
        copy(shard, slot, 0, a, x).wait_recv()

    def relay(k):
        source, target = ((x, y), (y, x))[k % 2]
        slot = slot_of(k, source)
        arrived(slot)
        start(out.at[:, slot], slot, a, target)

    for k in range(1, outer):
        start(shard, own, lax.rem(a + k, outer), b)
    mine = pltpu.make_async_copy(shard, out.at[:, own], local_sem)
    mine.start()
    for k in range(outer):
        slot = slot_of(k, b)
        source = shard
        if k:
            arrived(slot)
            source = out.at[:, slot]
        start(source, slot, a, x)
        start(source, slot, a, y)
        if k:
            relay(k - 1)
    relay(outer - 1)
    for k in range(outer):
        arrived(slot_of(k, (y, x)[k % 2]))
        arrived(slot_of(k, across))
    mine.wait()
    for one in started:
        one.wait_send()


def gather_kernel(outer, inner, own, out, shard, trade_sem, local_sem, send_sem, recv_sem):
    a, b, device = place(outer, inner)
    greet(outer, inner, a, b, device)
    trade(outer, inner, [(own, shard, trade_sem.at[0], trade_sem.at[1])])()
    gather(outer, inner, a, b, device, shard, out, local_sem, send_sem, recv_sem)


def update_kernel(
    outer, inner, part, weights, momentum, new_weights, new_momentum, out,
    near, mixed, sums, far, own16, near_send, near_recv, far_send, far_recv,
    local_sem, send_sem, recv_sem,
):
    a, b, device = place(outer, inner)
    greet(outer, inner, a, b, device)
    steps = list(range(1, outer)) + [0]
    x, y, across = sides(b)
    near_copies = {}

    def send_near(kind, j, src, peer):
        one = pltpu.make_async_remote_copy(
            src_ref=src,
            dst_ref=near.at[kind, j],
            send_sem=near_send.at[kind, j],
            recv_sem=near_recv.at[kind, j],
            device_id=device(a, peer),
            device_id_type=MESH,
        )
        one.start()
        near_copies[kind, j] = one

    def block(j, i):
        return lax.rem(a + j, outer) * inner + i

    for j in steps:
        first = (x, y)[j % 2]
        send_near(0, j, part.at[:, block(j, across)], first)
        send_near(1, j, part.at[:, block(j, first)], first)
    for j in steps:
        second = (y, x)[j % 2]
        near_copies[0, j].wait_recv()
        both = part[:, block(j, second)].astype(jnp.float32) + near[0, j].astype(jnp.float32)
        mixed[j] = both.astype(jnp.bfloat16)
        send_near(2, j, mixed.at[j], second)
    far_copies = []
    total = None
    for j in steps:
        target = lax.rem(a + j, outer)
        total = part[:, block(j, b)].astype(jnp.float32)
        for kind in (1, 2):
            near_copies[kind, j].wait_recv()
            total = total + near[kind, j].astype(jnp.float32)
        if j:
            sums[j - 1] = total.astype(jnp.bfloat16)
            one = pltpu.make_async_remote_copy(
                src_ref=sums.at[j - 1],
                dst_ref=far.at[j - 1],
                send_sem=far_send.at[j - 1],
                recv_sem=far_recv.at[j - 1],
                device_id=device(target, b),
                device_id_type=MESH,
            )
            one.start()
            far_copies.append(one)
    for j, one in enumerate(far_copies):
        one.wait_recv()
        total = total + far[j].astype(jnp.float32)
    fast = weights[...]
    moment = 0.9 * momentum[...] + total
    new_momentum[...] = moment
    moved = fast - moment
    keep_norm = jnp.sqrt(jnp.mean(fast * fast, axis=-1, keepdims=True))
    fresh = moved * keep_norm * lax.rsqrt(jnp.mean(moved * moved, axis=-1, keepdims=True) + 1e-06)
    new_weights[...] = fresh
    own16[...] = fresh.astype(jnp.bfloat16)
    gather(outer, inner, a, b, device, own16, out, local_sem, send_sem, recv_sem)
    for one in far_copies:
        one.wait_send()
    for one in near_copies.values():
        one.wait_send()


def gather_sems(outer, inner):
    return [
        pltpu.SemaphoreType.DMA,
        pltpu.SemaphoreType.DMA((outer - 1 + 3 * outer,)),
        pltpu.SemaphoreType.DMA((outer * inner,)),
    ]


def gathered(shard):
    outer, inner = group_shape(lax.axis_size("seq"))
    m, rows, width = shard.shape
    vmem = pl.BlockSpec(memory_space=pltpu.VMEM)
    out = pl.pallas_call(
        functools.partial(gather_kernel, outer, inner),
        out_shape=jax.ShapeDtypeStruct((m, outer * inner, rows, width), shard.dtype),
        in_specs=[vmem],
        out_specs=vmem,
        scratch_shapes=[pltpu.VMEM(shard.shape, shard.dtype), pltpu.SemaphoreType.DMA((2,))]
        + gather_sems(outer, inner),
        compiler_params=pltpu.CompilerParams(
            collective_id=0, has_side_effects=True, vmem_limit_bytes=32 * 2**20
        ),
        cost_estimate=pl.CostEstimate(flops=0, bytes_accessed=10**8, transcendentals=0),
    )(shard)
    return out.reshape(m, outer * inner * rows, width)


def updated(part, weights, momentum):
    outer, inner = group_shape(lax.axis_size("seq"))
    m, rows, width = weights.shape
    vmem = pl.BlockSpec(memory_space=pltpu.VMEM)
    block = (m, rows, width)
    dma = pltpu.SemaphoreType.DMA
    fresh, moment, out = pl.pallas_call(
        functools.partial(update_kernel, outer, inner),
        out_shape=(
            jax.ShapeDtypeStruct(block, jnp.float32),
            jax.ShapeDtypeStruct(block, jnp.float32),
            jax.ShapeDtypeStruct((m, outer * inner, rows, width), jnp.bfloat16),
        ),
        in_specs=[vmem] * 3,
        out_specs=(vmem,) * 3,
        scratch_shapes=[
            pltpu.VMEM((3, outer) + block, jnp.bfloat16),
            pltpu.VMEM((outer,) + block, jnp.bfloat16),
            pltpu.VMEM((outer - 1,) + block, jnp.bfloat16),
            pltpu.VMEM((outer - 1,) + block, jnp.bfloat16),
            pltpu.VMEM(block, jnp.bfloat16),
            dma((3, outer)),
            dma((3, outer)),
            dma((outer - 1,)),
            dma((outer - 1,)),
        ]
        + gather_sems(outer, inner),
        compiler_params=pltpu.CompilerParams(
            collective_id=1, has_side_effects=True, vmem_limit_bytes=40 * 2**20
        ),
        cost_estimate=pl.CostEstimate(flops=0, bytes_accessed=2 * 10**8, transcendentals=0),
    )(part, weights, momentum)
    return fresh, moment, out.reshape(m, outer * inner * rows, width)


def per_device(queries, key_rows, value_rows, step_rates, fast_weights, momentum, out_gain):
    tokens = queries.shape[0]
    head_dim = fast_weights.shape[2]
    size = lax.axis_size("seq")
    me = lax.axis_index("seq")
    first_core = me % 2 == 0
    grad_scale = 1.0 / math.sqrt(tokens * size)
    pair = [(i, i ^ 1) for i in range(size)]
    half = size // 2
    swap = []
    for i in range(size):
        head, m, core = i // half, (i % half) // 2, i % 2
        swap.append((i, core * half + m * 2 + head))
    start_rows = gathered(fast_weights.astype(jnp.bfloat16))
    state = jnp.stack([fast_weights, momentum])
    state, start_rows = lax.optimization_barrier((state, start_rows))
    held = lax.ppermute(state, "seq", swap)

    rates = jnp.repeat(step_rates.T, head_dim, axis=1)
    out_grad = (-grad_scale * rates * value_rows.astype(jnp.float32)).astype(jnp.bfloat16)
    whole = jnp.stack([key_rows, value_rows, out_grad, queries])
    low, high = whole[:, :, :head_dim], whole[:, :, head_dim:]
    kept = jnp.where(first_core, low, high)
    came = lax.ppermute(jnp.where(first_core, high, low), "seq", pair)
    mine = jnp.concatenate(
        [jnp.where(first_core, kept, came), jnp.where(first_core, came, kept)], axis=1
    )
    keys, values, outs, asks = mine[0], mine[1], mine[2], mine[3]

    reach = WINDOW // (2 * tokens)
    own_pair = mine[:2]
    window = [own_pair]
    if reach == 2:
        ahead = [(i, i + 4) for i in range(size - 4)]
        beside = [(i, i ^ 2) for i in range(size)]
        distant = lax.ppermute(own_pair, "seq", ahead)
        even_chip = (me // 2) % 2 == 0
        close = lax.ppermute(jnp.where(even_chip, own_pair, distant), "seq", beside)
        window = [distant, close, own_pair]
    else:
        for hop in range(1, reach + 1):
            route = [(i, i + 2 * hop) for i in range(size - 2 * hop)]
            window.insert(0, lax.ppermute(own_pair, "seq", route))

    key_gate = row_product(keys, start_rows[0])
    key_up = row_product(keys, start_rows[1])
    hidden_grad = row_product(outs, start_rows[2])
    key_hidden = (jax.nn.silu(key_gate) * key_up).astype(jnp.bfloat16)
    gate_grad = (hidden_grad * key_up * silu_slope(key_gate)).astype(jnp.bfloat16)
    up_grad = (hidden_grad * jax.nn.silu(key_gate)).astype(jnp.bfloat16)
    rows = fast_weights.shape[1]
    total = jnp.stack(
        [
            token_product(gate_grad, keys),
            token_product(up_grad, keys),
            token_product(key_hidden, outs),
        ]
    ).astype(jnp.bfloat16).reshape(3, half, rows, head_dim)
    new_weights, new_momentum, applied = updated(total, held[0], held[1])
    asks, applied = lax.optimization_barrier((asks, applied))
    base = jnp.reshape((me // 2) * (2 * tokens), (1,)).astype(jnp.int32)
    att_normed = window_attention(base, asks, window)
    owned = lax.ppermute(jnp.stack([new_weights, new_momentum]), "seq", swap)

    query_gate = row_product(asks, applied[0])
    query_up = row_product(asks, applied[1])
    query_hidden = (jax.nn.silu(query_gate) * query_up).astype(jnp.bfloat16)
    fast_out = jnp.dot(query_hidden, applied[2], preferred_element_type=jnp.float32)
    gain = jnp.where(first_core, out_gain[:head_dim], out_gain[head_dim:])
    fast_normed = (
        fast_out
        * lax.rsqrt(jnp.mean(fast_out * fast_out, axis=-1, keepdims=True) + 1e-06)
        * gain
    )
    layer = (fast_normed + att_normed).astype(jnp.bfloat16)
    early, late = layer[:tokens], layer[tokens:]
    stay = jnp.where(first_core, early, late)
    back = lax.ppermute(jnp.where(first_core, late, early), "seq", pair)
    layer_out = jnp.concatenate(
        [jnp.where(first_core, stay, back), jnp.where(first_core, back, stay)], axis=1
    )
    return (layer_out, owned[0], owned[1])


def solution(mesh):
    placed = (
        P(("groups", "seq"), None),
        P(("groups", "seq"), None),
        P(("groups", "seq"), None),
        P(None, ("groups", "seq")),
        P(None, "seq", None),
        P("groups", "seq", None),
        P(),
    )
    return jax.shard_map(
        per_device,
        mesh=mesh,
        in_specs=placed,
        out_specs=(P(("groups", "seq"), None), P("groups", "seq", None), P("groups", "seq", None)),
        check_vma=False,
    )
```

```python
import functools
import math

import jax
import jax.numpy as jnp
from jax import lax
from jax.experimental import pallas as pl
from jax.experimental.pallas import tpu as pltpu
from jax.sharding import PartitionSpec as P

ATT_DIM = 128
WINDOW = 1024


def silu_slope(values_in):
    sigmoid_val = jax.nn.sigmoid(values_in)
    return sigmoid_val * (1.0 + values_in * (1.0 - sigmoid_val))


def row_product(left_side, right_side):
    return lax.dot_general(
        left_side, right_side, (((1,), (1,)), ((), ())), preferred_element_type=jnp.float32
    )


def token_product(left_side, right_side):
    return lax.dot_general(
        left_side, right_side, (((0,), (0,)), ((), ())), preferred_element_type=jnp.float32
    )


def attention_kernel(tile, pieces, base_ref, q_ref, *refs):
    o_ref = refs[pieces]
    keys = jnp.concatenate([ref[0] for ref in refs[:pieces]], axis=0)
    values = jnp.concatenate([ref[1] for ref in refs[:pieces]], axis=0)
    tokens = q_ref.shape[0]
    span = tile + WINDOW
    base = base_ref[0]
    row = lax.broadcasted_iota(jnp.int32, (tile, span), 0)
    col = lax.broadcasted_iota(jnp.int32, (tile, span), 1)
    near = (col > row) & (col <= row + WINDOW)
    for lo in range(0, tokens, tile):
        scores = row_product(q_ref[lo : lo + tile, :], keys[lo : lo + span])
        scores = scores * (1.0 / math.sqrt(ATT_DIM))
        allowed = near & (col >= WINDOW - base - lo)
        scores = jnp.where(allowed, scores, -jnp.inf)
        exp_scores = jnp.exp(scores - jnp.max(scores, axis=-1, keepdims=True))
        total = jnp.sum(exp_scores, axis=-1, keepdims=True)
        attended = jnp.dot(
            exp_scores.astype(jnp.bfloat16),
            values[lo : lo + span],
            preferred_element_type=jnp.float32,
        ) / total
        mean = jnp.mean(attended * attended, axis=-1, keepdims=True)
        o_ref[lo : lo + tile, :] = attended * lax.rsqrt(mean + 1e-06)


def window_attention(base, q, window):
    tokens, width = q.shape
    tile = min(256, tokens)
    heads = width // ATT_DIM
    work = heads * tokens * (tile + WINDOW)
    pair = pl.BlockSpec((2, tokens, ATT_DIM), lambda a: (0, 0, a))
    return pl.pallas_call(
        functools.partial(attention_kernel, tile, len(window)),
        out_shape=jax.ShapeDtypeStruct((tokens, width), jnp.float32),
        grid=(heads,),
        in_specs=[
            pl.BlockSpec(memory_space=pltpu.SMEM),
            pl.BlockSpec((tokens, ATT_DIM), lambda a: (0, a)),
        ]
        + [pair] * len(window),
        out_specs=pl.BlockSpec((tokens, ATT_DIM), lambda a: (0, a)),
        compiler_params=pltpu.CompilerParams(vmem_limit_bytes=40 * 2**20),
        cost_estimate=pl.CostEstimate(
            flops=4 * work * ATT_DIM,
            bytes_accessed=4 * len(window) * tokens * width,
            transcendentals=work,
        ),
    )(base, q, *window)


MESH = pl.DeviceIdType.MESH


INNER = 4


def group_shape(size):
    return size // 2 // INNER, INNER


def sides(b):
    x = b + 1 - 2 * lax.rem(b, 2)
    return x, lax.rem(b + 2, INNER), lax.rem(x + 2, INNER)


def place(outer, inner):
    me = lax.axis_index("seq")
    core = lax.rem(me, 2)
    chip = lax.div(me, 2)
    return lax.div(chip, inner), lax.rem(chip, inner), lambda i, j: {"seq": (i * inner + j) * 2 + core}


def swap_partner(outer, inner):
    me = lax.axis_index("seq")
    half = outer * inner
    head, core = lax.div(me, half), lax.rem(me, 2)
    m = lax.div(lax.rem(me, half), 2)
    return head != core, head == core, {"seq": core * half + m * 2 + head}


def trade(outer, inner, moves):
    goes, stays, partner = swap_partner(outer, inner)

    def each(do_remote, do_local):
        @pl.when(goes)
        def _():
            for src, dst, send, recv in moves:
                do_remote(
                    pltpu.make_async_remote_copy(
                        src_ref=src,
                        dst_ref=dst,
                        send_sem=send,
                        recv_sem=recv,
                        device_id=partner,
                        device_id_type=MESH,
                    )
                )

        @pl.when(stays)
        def _():
            for src, dst, send, recv in moves:
                do_local(pltpu.make_async_copy(src, dst, recv))

    each(lambda one: one.start(), lambda one: one.start())
    return lambda: each(lambda one: one.wait(), lambda one: one.wait())


def greet(outer, inner, a, b, device):
    barrier = pltpu.get_barrier_semaphore()
    goes, stays, partner = swap_partner(outer, inner)

    @pl.when(goes)
    def _():
        pl.semaphore_signal(barrier, inc=1, device_id=partner, device_id_type=MESH)

    for k in range(1, outer):
        peer = device(lax.rem(a + k, outer), b)
        pl.semaphore_signal(barrier, inc=1, device_id=peer, device_id_type=MESH)
    for peer in sides(b)[:2]:
        pl.semaphore_signal(barrier, inc=1, device_id=device(a, peer), device_id_type=MESH)

    @pl.when(goes)
    def _():
        pl.semaphore_wait(barrier, outer + 2)

    @pl.when(stays)
    def _():
        pl.semaphore_wait(barrier, outer + 1)


def gather(outer, inner, a, b, device, shard, out, local_sem, send_sem, recv_sem):
    def copy(src, slot, send, i, j):
        return pltpu.make_async_remote_copy(
            src_ref=src,
            dst_ref=out.at[:, slot],
            send_sem=send_sem.at[send],
            recv_sem=recv_sem.at[slot],
            device_id=device(i, j),
            device_id_type=MESH,
        )

    own = a * inner + b
    started = []

    def start(src, slot, i, j):
        one = copy(src, slot, len(started), i, j)
        one.start()
        started.append(one)

    x, y, across = sides(b)

    def slot_of(k, i):
        return lax.rem(a + k, outer) * inner + i

    def arrived(slot):
        copy(shard, slot, 0, a, x).wait_recv()

    def relay(k):
        source, target = ((x, y), (y, x))[k % 2]
        slot = slot_of(k, source)
        arrived(slot)
        start(out.at[:, slot], slot, a, target)

    for k in range(1, outer):
        start(shard, own, lax.rem(a + k, outer), b)
    mine = pltpu.make_async_copy(shard, out.at[:, own], local_sem)
    mine.start()
    for k in range(outer):
        slot = slot_of(k, b)
        source = shard
        if k:
            arrived(slot)
            source = out.at[:, slot]
        start(source, slot, a, x)
        start(source, slot, a, y)
        if k:
            relay(k - 1)
    relay(outer - 1)
    for k in range(outer):
        arrived(slot_of(k, (y, x)[k % 2]))
        arrived(slot_of(k, across))
    mine.wait()
    for one in started:
        one.wait_send()


def gather_kernel(outer, inner, own, out, shard, trade_sem, local_sem, send_sem, recv_sem):
    a, b, device = place(outer, inner)
    greet(outer, inner, a, b, device)
    trade(outer, inner, [(own, shard, trade_sem.at[0], trade_sem.at[1])])()
    gather(outer, inner, a, b, device, shard, out, local_sem, send_sem, recv_sem)


def update_kernel(
    outer, inner, part, weights, momentum, new_weights, new_momentum, out,
    near, mixed, sums, far, own16, near_send, near_recv, far_send, far_recv,
    local_sem, send_sem, recv_sem,
):
    a, b, device = place(outer, inner)
    greet(outer, inner, a, b, device)
    steps = list(range(1, outer)) + [0]
    x, y, across = sides(b)
    near_copies = {}

    def send_near(kind, j, src, peer):
        one = pltpu.make_async_remote_copy(
            src_ref=src,
            dst_ref=near.at[kind, j],
            send_sem=near_send.at[kind, j],
            recv_sem=near_recv.at[kind, j],
            device_id=device(a, peer),
            device_id_type=MESH,
        )
        one.start()
        near_copies[kind, j] = one

    def block(j, i):
        return lax.rem(a + j, outer) * inner + i

    for j in steps:
        first = (x, y)[j % 2]
        send_near(0, j, part.at[:, block(j, across)], first)
        send_near(1, j, part.at[:, block(j, first)], first)
    for j in steps:
        second = (y, x)[j % 2]
        near_copies[0, j].wait_recv()
        both = part[:, block(j, second)].astype(jnp.float32) + near[0, j].astype(jnp.float32)
        mixed[j] = both.astype(jnp.bfloat16)
        send_near(2, j, mixed.at[j], second)
    far_copies = []
    total = None
    for j in steps:
        target = lax.rem(a + j, outer)
        total = part[:, block(j, b)].astype(jnp.float32)
        for kind in (1, 2):
            near_copies[kind, j].wait_recv()
            total = total + near[kind, j].astype(jnp.float32)
        if j:
            sums[j - 1] = total.astype(jnp.bfloat16)
            one = pltpu.make_async_remote_copy(
                src_ref=sums.at[j - 1],
                dst_ref=far.at[j - 1],
                send_sem=far_send.at[j - 1],
                recv_sem=far_recv.at[j - 1],
                device_id=device(target, b),
                device_id_type=MESH,
            )
            one.start()
            far_copies.append(one)
    for j, one in enumerate(far_copies):
        one.wait_recv()
        total = total + far[j].astype(jnp.float32)
    fast = weights[...]
    moment = 0.9 * momentum[...] + total
    new_momentum[...] = moment
    moved = fast - moment
    keep_norm = jnp.sqrt(jnp.mean(fast * fast, axis=-1, keepdims=True))
    fresh = moved * keep_norm * lax.rsqrt(jnp.mean(moved * moved, axis=-1, keepdims=True) + 1e-06)
    new_weights[...] = fresh
    own16[...] = fresh.astype(jnp.bfloat16)
    gather(outer, inner, a, b, device, own16, out, local_sem, send_sem, recv_sem)
    for one in far_copies:
        one.wait_send()
    for one in near_copies.values():
        one.wait_send()


def gather_sems(outer, inner):
    return [
        pltpu.SemaphoreType.DMA,
        pltpu.SemaphoreType.DMA((outer - 1 + 3 * outer,)),
        pltpu.SemaphoreType.DMA((outer * inner,)),
    ]


def gathered(shard):
    outer, inner = group_shape(lax.axis_size("seq"))
    m, rows, width = shard.shape
    vmem = pl.BlockSpec(memory_space=pltpu.VMEM)
    out = pl.pallas_call(
        functools.partial(gather_kernel, outer, inner),
        out_shape=jax.ShapeDtypeStruct((m, outer * inner, rows, width), shard.dtype),
        in_specs=[vmem],
        out_specs=vmem,
        scratch_shapes=[pltpu.VMEM(shard.shape, shard.dtype), pltpu.SemaphoreType.DMA((2,))]
        + gather_sems(outer, inner),
        compiler_params=pltpu.CompilerParams(
            collective_id=0, has_side_effects=True, vmem_limit_bytes=32 * 2**20
        ),
        cost_estimate=pl.CostEstimate(flops=0, bytes_accessed=10**8, transcendentals=0),
    )(shard)
    return out.reshape(m, outer * inner * rows, width)


def updated(part, weights, momentum):
    outer, inner = group_shape(lax.axis_size("seq"))
    m, rows, width = weights.shape
    vmem = pl.BlockSpec(memory_space=pltpu.VMEM)
    block = (m, rows, width)
    dma = pltpu.SemaphoreType.DMA
    fresh, moment, out = pl.pallas_call(
        functools.partial(update_kernel, outer, inner),
        out_shape=(
            jax.ShapeDtypeStruct(block, jnp.float32),
            jax.ShapeDtypeStruct(block, jnp.float32),
            jax.ShapeDtypeStruct((m, outer * inner, rows, width), jnp.bfloat16),
        ),
        in_specs=[vmem] * 3,
        out_specs=(vmem,) * 3,
        scratch_shapes=[
            pltpu.VMEM((3, outer) + block, jnp.bfloat16),
            pltpu.VMEM((outer,) + block, jnp.bfloat16),
            pltpu.VMEM((outer - 1,) + block, jnp.bfloat16),
            pltpu.VMEM((outer - 1,) + block, jnp.bfloat16),
            pltpu.VMEM(block, jnp.bfloat16),
            dma((3, outer)),
            dma((3, outer)),
            dma((outer - 1,)),
            dma((outer - 1,)),
        ]
        + gather_sems(outer, inner),
        compiler_params=pltpu.CompilerParams(
            collective_id=1, has_side_effects=True, vmem_limit_bytes=40 * 2**20
        ),
        cost_estimate=pl.CostEstimate(flops=0, bytes_accessed=2 * 10**8, transcendentals=0),
    )(part, weights, momentum)
    return fresh, moment, out.reshape(m, outer * inner * rows, width)


def per_device(queries, key_rows, value_rows, step_rates, fast_weights, momentum, out_gain):
    tokens = queries.shape[0]
    head_dim = fast_weights.shape[2]
    size = lax.axis_size("seq")
    me = lax.axis_index("seq")
    first_core = me % 2 == 0
    grad_scale = 1.0 / math.sqrt(tokens * size)
    pair = [(i, i ^ 1) for i in range(size)]
    half = size // 2
    swap = []
    for i in range(size):
        head, m, core = i // half, (i % half) // 2, i % 2
        swap.append((i, core * half + m * 2 + head))

    rates = jnp.repeat(step_rates.T, head_dim, axis=1)
    out_grad = (-grad_scale * rates * value_rows.astype(jnp.float32)).astype(jnp.bfloat16)
    whole = jnp.stack([key_rows, value_rows, out_grad, queries])
    low, high = whole[:, :, :head_dim], whole[:, :, head_dim:]
    kept = jnp.where(first_core, low, high)
    came = lax.ppermute(jnp.where(first_core, high, low), "seq", pair)
    mine = jnp.concatenate(
        [jnp.where(first_core, kept, came), jnp.where(first_core, came, kept)], axis=1
    )
    keys, values, outs, asks = mine[0], mine[1], mine[2], mine[3]

    state = jnp.stack([fast_weights, momentum])
    reach = WINDOW // (2 * tokens)
    start_rows = gathered(fast_weights.astype(jnp.bfloat16))
    own_pair = mine[:2]
    window = [own_pair]
    if reach == 2:
        ahead = [(i, i + 4) for i in range(size - 4)]
        beside = [(i, i ^ 2) for i in range(size)]
        distant = lax.ppermute(own_pair, "seq", ahead)
        state, distant = lax.optimization_barrier((state, distant))
        even_chip = (me // 2) % 2 == 0
        close = lax.ppermute(jnp.where(even_chip, own_pair, distant), "seq", beside)
        window = [distant, close, own_pair]
    else:
        for hop in range(1, reach + 1):
            route = [(i, i + 2 * hop) for i in range(size - 2 * hop)]
            window.insert(0, lax.ppermute(own_pair, "seq", route))

    held = lax.ppermute(state, "seq", swap)
    key_gate = row_product(keys, start_rows[0])
    key_up = row_product(keys, start_rows[1])
    hidden_grad = row_product(outs, start_rows[2])
    key_hidden = (jax.nn.silu(key_gate) * key_up).astype(jnp.bfloat16)
    gate_grad = (hidden_grad * key_up * silu_slope(key_gate)).astype(jnp.bfloat16)
    up_grad = (hidden_grad * jax.nn.silu(key_gate)).astype(jnp.bfloat16)
    rows = fast_weights.shape[1]
    total = jnp.stack(
        [
            token_product(gate_grad, keys),
            token_product(up_grad, keys),
            token_product(key_hidden, outs),
        ]
    ).astype(jnp.bfloat16).reshape(3, half, rows, head_dim)
    new_weights, new_momentum, applied = updated(total, held[0], held[1])
    asks, applied = lax.optimization_barrier((asks, applied))
    base = jnp.reshape((me // 2) * (2 * tokens), (1,)).astype(jnp.int32)
    att_normed = window_attention(base, asks, window)
    owned = lax.ppermute(jnp.stack([new_weights, new_momentum]), "seq", swap)

    query_gate = row_product(asks, applied[0])
    query_up = row_product(asks, applied[1])
    query_hidden = (jax.nn.silu(query_gate) * query_up).astype(jnp.bfloat16)
    fast_out = jnp.dot(query_hidden, applied[2], preferred_element_type=jnp.float32)
    gain = jnp.where(first_core, out_gain[:head_dim], out_gain[head_dim:])
    fast_normed = (
        fast_out
        * lax.rsqrt(jnp.mean(fast_out * fast_out, axis=-1, keepdims=True) + 1e-06)
        * gain
    )
    layer = (fast_normed + att_normed).astype(jnp.bfloat16)
    early, late = layer[:tokens], layer[tokens:]
    stay = jnp.where(first_core, early, late)
    back = lax.ppermute(jnp.where(first_core, late, early), "seq", pair)
    layer_out = jnp.concatenate(
        [jnp.where(first_core, stay, back), jnp.where(first_core, back, stay)], axis=1
    )
    return (layer_out, owned[0], owned[1])


def solution(mesh):
    placed = (
        P(("groups", "seq"), None),
        P(("groups", "seq"), None),
        P(("groups", "seq"), None),
        P(None, ("groups", "seq")),
        P(None, "seq", None),
        P("groups", "seq", None),
        P(),
    )
    return jax.shard_map(
        per_device,
        mesh=mesh,
        in_specs=placed,
        out_specs=(P(("groups", "seq"), None), P("groups", "seq", None), P("groups", "seq", None)),
        check_vma=False,
    )
```
